32 devices in a mesh: ctx: 8 (over z, x), ch: 4 (over y, core).
Axes of the slice: x: 2, y: 2, z: 4, core: 2. Of those that a mesh axis runs over, the one named last changes fastest.
Arguments:
- q_conv: bfloat16 [1792, 4096], P('ctx', 'ch'), may hold values from -6 to 6
- k_conv: bfloat16 [1792, 4096], P('ctx', 'ch'), may hold values from -6 to 6
- v_conv: bfloat16 [1792, 4096], P('ctx', 'ch'), may hold values from -6 to 6
- conv_filter: bfloat16 [1792, 256], P('ctx', 'ch'), may hold values from -1 to 1
- q_attn: bfloat16 [1792, 4096], P('ctx', 'ch'), may hold values from -5 to 5
- k_attn: bfloat16 [1792, 4096], P('ctx', 'ch'), may hold values from -5 to 5
- v_attn: bfloat16 [1792, 4096], P('ctx', 'ch'), may hold values from -6 to 6
- w_conv_out: bfloat16 [4096, 4096], P('ch'), may hold values from -0.09375 to 0.09375
- w_attn_out: bfloat16 [4096, 4096], P('ch'), may hold values from -0.375 to 0.375
Outputs:
- layer_out: bfloat16 [1792, 4096], P(('ctx', 'ch'))
The draws below stay inside these ranges and needn't reach their ends.
All inputs are finite; a program needn't handle non-finite values.
Results may differ from the reference program's by a relative error of at most 0.018.
Values may be sent and summed in bfloat16 or wider, within the bound.
A program may use at most 192 MiB of HBM per device.

```python
import math
import jax
import jax.numpy as jnp
from jax import lax

CH = 4096
GSIZE = 16
FILTER_GROUPS = 256
HEADS = 32
HD = 128
DOUT = 4096
BLK = 224
SEQUENCE_TOKENS = 1792


def attention_pair(base_key):
    width_all = HEADS * HD
    query_key = jax.random.fold_in(base_key, 11)
    keys_key = jax.random.fold_in(base_key, 12)
    queries = jnp.clip(1.4 * jax.random.normal(query_key, (SEQUENCE_TOKENS, width_all), jnp.float32), -5.0, 5.0)
    keys_drawn = jnp.clip(1.4 * jax.random.normal(keys_key, (SEQUENCE_TOKENS, width_all), jnp.float32), -5.0, 5.0)
    return (queries, keys_drawn)


def draw_q_attn(key, part):
    return attention_pair(key)[0].astype(jnp.bfloat16)


def draw_k_attn(key, part):
    return attention_pair(key)[1].astype(jnp.bfloat16)


def draw_conv_filter(key, part):
    choose_key = jax.random.fold_in(key, 21)
    slow_key = jax.random.fold_in(key, 22)
    fast_key = jax.random.fold_in(key, 23)
    noise_key = jax.random.fold_in(key, 24)
    spike_random_key = jax.random.fold_in(key, 25)
    retain_random_key = jax.random.fold_in(key, 26)
    time_positions = jnp.arange(SEQUENCE_TOKENS, dtype=jnp.float32)[:, None]
    choose = jax.random.bernoulli(choose_key, 0.5, (1, FILTER_GROUPS))
    slow_rates = jnp.exp(jax.random.uniform(slow_key, (1, FILTER_GROUPS), jnp.float32, math.log(0.1 / SEQUENCE_TOKENS), math.log(2.0 / SEQUENCE_TOKENS)))
    fast_rates = jnp.exp(jax.random.uniform(fast_key, (1, FILTER_GROUPS), jnp.float32, math.log(2.0 / SEQUENCE_TOKENS), math.log(1.0 / 30.0)))
    decay_rates = jnp.where(choose, slow_rates, fast_rates)
    noise_vals = jax.random.normal(noise_key, (SEQUENCE_TOKENS, FILTER_GROUPS), jnp.float32)
    spike_positions = jax.random.randint(spike_random_key, (3, 1, FILTER_GROUPS), 1, SEQUENCE_TOKENS)
    spike_retained = jax.random.uniform(retain_random_key, (3, 1, FILTER_GROUPS), jnp.float32, 0.5, 0.8)
    log_envelope = -decay_rates * time_positions
    for spike_total in range(3):
        elapsed_offsets = (time_positions >= spike_positions[spike_total].astype(jnp.float32)).astype(jnp.float32)
        log_envelope = log_envelope + jnp.log(spike_retained[spike_total]) * elapsed_offsets
    norm_factor = jnp.sqrt((1.0 - jnp.exp(-2.0 * decay_rates)) / (1.0 - jnp.exp(-2.0 * decay_rates * SEQUENCE_TOKENS)))
    values = jnp.clip(noise_vals, -4.0, 4.0) * jnp.exp(log_envelope) * norm_factor
    values = jnp.clip(values, -1.0, 1.0)
    values = values.at[0, 0].set(1.0)
    values = values.at[0, 1].set(-1.0)
    return values.astype(jnp.bfloat16)


def steps_of(key, dims, shards, least, top_value):
    def one(dim, blocks):
        heights = jax.random.uniform(jax.random.fold_in(jax.random.fold_in(key, 6), dim), (blocks,), jnp.float32, least / len(shards), top_value / len(shards))
        return jnp.repeat(jnp.exp(heights), dims[dim] // blocks).reshape((-1,) + (1,) * (len(dims) - dim - 1))

    loudness = one(*shards[0])
    for cut in shards[1:]:
        loudness = loudness * one(*cut)
    return loudness


def normal_values(rng, dims, scale, bound, cuts=(), kind=jnp.bfloat16):
    level = steps_of(rng, dims, cuts, -0.22, 0.18) if cuts else 1.0
    drawn = jax.random.normal(rng, dims, jnp.float32) * scale * level
    return jnp.minimum(jnp.maximum(drawn, -bound), bound).astype(kind)


def setup_inputs(seed: int = 0) -> dict:
    key_of = jax.random.split(jax.random.key(seed), 10)
    q_conv = normal_values(key_of[0], (SEQUENCE_TOKENS, CH), 1.0, 6.0, ((0, 8), (1, 4)))
    k_conv = normal_values(key_of[1], (SEQUENCE_TOKENS, CH), 1.0, 6.0, ((0, 8), (1, 4)))
    v_conv = normal_values(key_of[2], (SEQUENCE_TOKENS, CH), 1.0, 6.0, ((0, 8), (1, 4)))
    conv_filter = draw_conv_filter(jax.random.fold_in(key_of[9], 71), 0)
    q_attn = draw_q_attn(jax.random.fold_in(key_of[9], 71), 0)
    k_attn = draw_k_attn(jax.random.fold_in(key_of[9], 71), 0)
    v_attn = normal_values(key_of[6], (SEQUENCE_TOKENS, HEADS * HD), 1.0, 6.0, ((0, 8), (1, 4)))
    w_conv_out = normal_values(key_of[7], (CH, DOUT), CH ** -0.5, 0.09375, ((0, 4),))
    w_attn_out = normal_values(key_of[8], (HEADS * HD, DOUT), (2 * HD) ** -0.5, 0.375, ((0, 4),))
    return {"q_conv": q_conv, "k_conv": k_conv, "v_conv": v_conv, "conv_filter": conv_filter, "q_attn": q_attn, "k_attn": k_attn, "v_attn": v_attn, "w_conv_out": w_conv_out, "w_attn_out": w_attn_out}


def head_attention(packed):
    query_head, key_head, value_head = packed
    key_pos = jnp.arange(SEQUENCE_TOKENS, dtype=jnp.int32)
    key_wide = key_head.astype(jnp.float32)
    value_wide = value_head.astype(jnp.float32)

    def block_attention(block_number):
        first_row = block_number * BLK
        query_block = lax.dynamic_slice_in_dim(query_head, first_row, BLK, 0).astype(jnp.float32)
        scores = jnp.dot(query_block, key_wide.T, preferred_element_type=jnp.float32) * (HD ** -0.5)
        query_pos = first_row + jnp.arange(BLK, dtype=jnp.int32)
        allowed = key_pos[None, :] <= query_pos[:, None]
        row_max = jnp.max(jnp.where(allowed, scores, jnp.float32(-1e30)), axis=1, keepdims=True)
        weights = jnp.where(allowed, jnp.exp(scores - row_max), jnp.float32(0.0))
        totals = jnp.sum(weights, axis=1, keepdims=True)
        rounded = weights.astype(jnp.bfloat16).astype(jnp.float32)
        return jnp.dot(rounded, value_wide, preferred_element_type=jnp.float32) / totals

    blocks = lax.map(block_attention, jnp.arange(SEQUENCE_TOKENS // BLK, dtype=jnp.int32))
    return blocks.reshape(SEQUENCE_TOKENS, HD)


def reference(q_conv, k_conv, v_conv, conv_filter, q_attn, k_attn, v_attn, w_conv_out, w_attn_out):
    gated = (k_conv.astype(jnp.float32) * v_conv.astype(jnp.float32)).astype(jnp.bfloat16)
    length_all = 2 * SEQUENCE_TOKENS
    source_spec = jnp.fft.rfft(gated.astype(jnp.float32), n=length_all, axis=0)
    filter_spec = jnp.fft.rfft(conv_filter.astype(jnp.float32), n=length_all, axis=0)
    product = source_spec.reshape(-1, FILTER_GROUPS, GSIZE) * filter_spec[:, :, None]
    conv = jnp.fft.irfft(product.reshape(-1, CH), n=length_all, axis=0)[:SEQUENCE_TOKENS].astype(jnp.bfloat16)
    mixed = (q_conv.astype(jnp.float32) * conv.astype(jnp.float32)).astype(jnp.bfloat16)
    stacked = (q_attn.reshape(SEQUENCE_TOKENS, HEADS, HD).transpose(1, 0, 2),
               k_attn.reshape(SEQUENCE_TOKENS, HEADS, HD).transpose(1, 0, 2),
               v_attn.reshape(SEQUENCE_TOKENS, HEADS, HD).transpose(1, 0, 2))
    per_head = lax.map(head_attention, stacked)
    attended = per_head.transpose(1, 0, 2).reshape(SEQUENCE_TOKENS, HEADS * HD).astype(jnp.bfloat16)
    summed = jnp.dot(mixed, w_conv_out, preferred_element_type=jnp.float32) + jnp.dot(attended, w_attn_out, preferred_element_type=jnp.float32)
    return summed.astype(jnp.bfloat16)
```

```python
from functools import partial
import math

import jax
import jax.numpy as jnp
from jax import lax
from jax.experimental import pallas as pl
from jax.experimental.pallas import tpu as pltpu
from jax.sharding import PartitionSpec as P

HD = 128


two_pi = 2.0 * math.pi
neg_large = -1e30
highest = lax.Precision.HIGHEST


def angle_table(left_idx, right_idx, period):
    product = left_idx[:, None] * right_idx[None, :] % period
    return product.astype(jnp.float32) * (two_pi / period)


def section_coarse(values, cos_table, sin_table, twiddle):
    real_part = jnp.einsum("kn,nsc->ksc", cos_table, values, precision=highest)
    imag_part = -jnp.einsum("kn,nsc->ksc", sin_table, values, precision=highest)
    cos_twist = jnp.cos(twiddle)[:, :, None]
    sin_twist = jnp.sin(twiddle)[:, :, None]
    return (
        real_part * cos_twist + imag_part * sin_twist,
        imag_part * cos_twist - real_part * sin_twist,
    )


def section_fine(real_part, imag_part, cos_table, sin_table, direction):
    cos_real = jnp.einsum("kn,anc->akc", cos_table, real_part, precision=highest)
    cos_imag = jnp.einsum("kn,anc->akc", cos_table, imag_part, precision=highest)
    sin_real = jnp.einsum("kn,anc->akc", sin_table, real_part, precision=highest)
    sin_imag = jnp.einsum("kn,anc->akc", sin_table, imag_part, precision=highest)
    return (cos_real - direction * sin_imag, cos_imag + direction * sin_real)


def spectral_conv(gated, filters, my_index, tok_rows, count_ctx):
    chans = gated.shape[1]
    groups = filters.shape[1]
    share = chans // groups
    sub_rows = tok_rows // count_ctx
    period = 2 * count_ctx * tok_rows
    got_source, got_filter = (
        lax.all_to_all(
            gated.reshape(1, tok_rows, chans), "ctx", split_axis=1, concat_axis=0, tiled=True
        ),
        lax.all_to_all(
            filters.reshape(1, tok_rows, groups), "ctx", split_axis=1, concat_axis=0, tiled=True
        ),
    )
    coarse_idx = jnp.arange(count_ctx, dtype=jnp.int32)
    coarse_freq = jnp.arange(2 * count_ctx, dtype=jnp.int32)
    coarse_angle = angle_table(coarse_freq, coarse_idx, 2 * count_ctx)
    cos_coarse = jnp.cos(coarse_angle)
    sin_coarse = jnp.sin(coarse_angle)
    fine_global = my_index * sub_rows + jnp.arange(sub_rows, dtype=jnp.int32)
    twist_in = angle_table(coarse_freq, fine_global, period)
    source_re, source_im = section_coarse(
        got_source.astype(jnp.float32), cos_coarse, sin_coarse, twist_in
    )
    filter_re, filter_im = section_coarse(
        got_filter.astype(jnp.float32), cos_coarse, sin_coarse, twist_in
    )
    source_re, source_im, filter_re, filter_im = (
        lax.all_to_all(
            source_re.astype(jnp.bfloat16), "ctx", split_axis=0, concat_axis=1, tiled=True
        ).astype(source_re.dtype),
        lax.all_to_all(
            source_im.astype(jnp.bfloat16), "ctx", split_axis=0, concat_axis=1, tiled=True
        ).astype(source_im.dtype),
        lax.all_to_all(
            filter_re.astype(jnp.bfloat16), "ctx", split_axis=0, concat_axis=1, tiled=True
        ).astype(filter_re.dtype),
        lax.all_to_all(
            filter_im.astype(jnp.bfloat16), "ctx", split_axis=0, concat_axis=1, tiled=True
        ).astype(filter_im.dtype),
    )
    fine_idx = jnp.arange(tok_rows, dtype=jnp.int32)
    fine_angle = angle_table(fine_idx, fine_idx, tok_rows)
    cos_fine = jnp.cos(fine_angle)
    sin_fine = jnp.sin(fine_angle)
    source_re, source_im = section_fine(source_re, source_im, cos_fine, sin_fine, -1.0)
    filter_re, filter_im = section_fine(filter_re, filter_im, cos_fine, sin_fine, -1.0)
    split_re = source_re.reshape(2, tok_rows, groups, share)
    split_im = source_im.reshape(2, tok_rows, groups, share)
    prod_re = split_re * filter_re[..., None] - split_im * filter_im[..., None]
    prod_im = split_re * filter_im[..., None] + split_im * filter_re[..., None]
    back_re, back_im = section_fine(
        prod_re.reshape(2, tok_rows, chans),
        prod_im.reshape(2, tok_rows, chans),
        cos_fine,
        sin_fine,
        1.0,
    )
    pair_freq = my_index * 2 + jnp.arange(2, dtype=jnp.int32)
    twist_out = angle_table(pair_freq, fine_idx, period)
    cos_out = jnp.cos(twist_out)[:, :, None]
    sin_out = jnp.sin(twist_out)[:, :, None]
    turned_re = back_re * cos_out - back_im * sin_out
    turned_im = back_re * sin_out + back_im * cos_out
    turned_re, turned_im = (
        lax.all_to_all(
            turned_re.astype(jnp.bfloat16), "ctx", split_axis=1, concat_axis=0, tiled=True
        ).astype(turned_re.dtype),
        lax.all_to_all(
            turned_im.astype(jnp.bfloat16), "ctx", split_axis=1, concat_axis=0, tiled=True
        ).astype(turned_im.dtype),
    )
    result = jnp.einsum("nk,ksc->nsc", cos_coarse.T, turned_re, precision=highest)
    result = result - jnp.einsum("nk,ksc->nsc", sin_coarse.T, turned_im, precision=highest)
    rounded = (result / period).astype(jnp.bfloat16)
    returned = lax.all_to_all(rounded, "ctx", split_axis=0, concat_axis=1, tiled=True)
    return returned.reshape(tok_rows, chans)


def keep_same(running):
    return running


def attend_block(group_query, group_pos, key_block, value_block, key_pos, score_scale, group_state):
    run_max, run_total, run_accum = group_state
    scores = (
        jnp.einsum("thd,shd->hts", group_query, key_block, preferred_element_type=jnp.float32)
        * score_scale
    )
    allowed = (key_pos[None, :] <= group_pos[:, None])[None]
    block_max = jnp.max(jnp.where(allowed, scores, neg_large), axis=2)
    new_max = jnp.maximum(run_max, block_max)
    factor = jnp.exp(run_max - new_max)
    weights = jnp.where(allowed, jnp.exp(scores - new_max[:, :, None]), 0.0)
    new_total = run_total * factor + jnp.sum(weights, axis=2)
    new_accum = run_accum * factor[:, :, None] + jnp.einsum(
        "hts,shd->htd",
        weights.astype(jnp.bfloat16),
        value_block,
        preferred_element_type=jnp.float32,
    )
    return (new_max, new_total, new_accum)


def attention(q_attn, k_attn, v_attn, my_index, tok_rows):
    heads_local = q_attn.shape[1] // HD
    score_scale = HD ** (-0.5)
    queries = q_attn.reshape(tok_rows, heads_local, HD)
    group_list = [(queries, my_index * tok_rows + jnp.arange(tok_rows, dtype=jnp.int32))]
    initial = tuple(
        (
            (
                jnp.full((heads_local, entry[0].shape[0]), neg_large, jnp.float32),
                jnp.zeros((heads_local, entry[0].shape[0]), jnp.float32),
                jnp.zeros((heads_local, entry[0].shape[0], HD), jnp.float32),
            )
            for entry in group_list
        )
    )
    key_piece = lax.all_gather(k_attn, "ctx", axis=0, tiled=True)
    value_piece = lax.all_gather(v_attn, "ctx", axis=0, tiled=True)
    count_blocks = key_piece.shape[0] // tok_rows
    keys_split = key_piece.reshape(count_blocks, tok_rows, heads_local, HD)
    values_split = value_piece.reshape(count_blocks, tok_rows, heads_local, HD)

    def one_block(carry, item):
        key_block, value_block, block_number = item
        block_first = block_number * tok_rows
        key_pos = block_first + jnp.arange(tok_rows, dtype=jnp.int32)
        updated = []
        for entry, group_state in zip(group_list, carry):
            step_fn = partial(
                attend_block, entry[0], entry[1], key_block, value_block, key_pos, score_scale
            )
            updated.append(lax.cond(block_first <= entry[1][-1], step_fn, keep_same, group_state))
        return (tuple(updated), None)

    new_state, unused = lax.scan(
        one_block, initial, (keys_split, values_split, jnp.arange(count_blocks, dtype=jnp.int32))
    )
    outputs = [
        (state[2] / state[1][:, :, None]).transpose(1, 0, 2).astype(jnp.bfloat16)
        for state in new_state
    ]
    merged = outputs[0]
    return merged.reshape(tok_rows, heads_local * HD)


def local_general(q_conv, k_conv, v_conv, conv_filter, q_attn, k_attn, v_attn, w_conv_out, w_attn_out):
    count_ctx = lax.axis_size("ctx")
    my_index = lax.axis_index("ctx")
    tok_rows = q_conv.shape[0]
    gated = (k_conv.astype(jnp.float32) * v_conv.astype(jnp.float32)).astype(jnp.bfloat16)
    conv = spectral_conv(gated, conv_filter, my_index, tok_rows, count_ctx)
    mixed = (q_conv.astype(jnp.float32) * conv.astype(jnp.float32)).astype(jnp.bfloat16)
    attended = attention(q_attn, k_attn, v_attn, my_index, tok_rows)
    return lax.psum_scatter(
        (
            jnp.dot(mixed, w_conv_out, preferred_element_type=jnp.float32)
            + jnp.dot(attended, w_attn_out, preferred_element_type=jnp.float32)
        ).astype(jnp.bfloat16),
        "ch",
        scatter_dimension=0,
        tiled=True,
    )


GROUP = 16
TILE = 256
HALF = 128
MESH = pl.DeviceIdType.MESH


def fused_kernel(
    count_ctx, rows, width,
    qc_ref, kc_ref, vc_ref, filt_ref, q_ref, k_ref, v_ref, w1_hbm, w2_hbm,
    out_ref,
    gated, filt_in, gated_in, q_in, k_in, v_in, conv_out, attn_out, conv_back, attn_back,
    fpad, x_turned, y_turned, stage, lhs_conv, lhs_attn, w1, w2,
    keep, send_a, recv_a, send_b, recv_b,
    in_send, in_recv, back_send, back_recv, w_sem, a_send, a_recv, b_send, b_recv,
):
    me = lax.axis_index("ctx")
    ch = lax.axis_index("ch")
    core = lax.rem(ch, 2)
    pair = ch // 2
    core_peer = pair * 2 + (1 - core)
    pair_peer = (1 - pair) * 2 + core
    tokens = count_ctx * rows
    tiles = tokens // TILE
    groups = HD // GROUP

    w1_copy = pltpu.make_async_copy(w1_hbm, w1, w_sem.at[0])
    w2_copy = pltpu.make_async_copy(w2_hbm, w2, w_sem.at[1])
    w1_copy.start()
    w2_copy.start()

    barrier = pltpu.get_barrier_semaphore()
    for k in range(1, count_ctx):
        peer = lax.rem(me + k, count_ctx)
        pl.semaphore_signal(barrier, inc=1, device_id=(peer, ch), device_id_type=MESH)
    pl.semaphore_signal(barrier, inc=1, device_id=(me, core_peer), device_id_type=MESH)
    pl.semaphore_signal(barrier, inc=1, device_id=(me, pair_peer), device_id_type=MESH)

    gated[...] = (kc_ref[...].astype(jnp.float32) * vc_ref[...].astype(jnp.float32)).astype(
        jnp.bfloat16
    )
    pl.semaphore_wait(barrier, count_ctx + 1)

    my_rows = pl.ds(pl.multiple_of(me * rows, 16), rows)
    my_cols = pl.ds(pl.multiple_of(me * HD, HD), HD)
    my_groups = pl.ds(pl.multiple_of(me * groups, groups), groups)
    pieces = ((gated, gated_in), (q_ref, q_in), (k_ref, k_in), (v_ref, v_in))
    inbound = [[] for unused in range(5)]
    for k in range(1, count_ctx):
        peer = lax.rem(me + k, count_ctx)
        peer_groups = pl.ds(pl.multiple_of(peer * groups, groups), groups)
        copy = pltpu.make_async_remote_copy(
            src_ref=filt_ref.at[peer_groups, :],
            dst_ref=filt_in.at[me],
            send_sem=in_send.at[4, k],
            recv_sem=in_recv.at[4, k],
            device_id=(peer, ch),
            device_id_type=MESH,
        )
        copy.start()
        inbound[4].append(copy)
    for number, (source, target) in enumerate(pieces):
        for k in range(1, count_ctx):
            peer = lax.rem(me + k, count_ctx)
            peer_cols = pl.ds(pl.multiple_of(peer * HD, HD), HD)
            copy = pltpu.make_async_remote_copy(
                src_ref=source.at[:, peer_cols],
                dst_ref=target.at[my_rows, :],
                send_sem=in_send.at[number, k],
                recv_sem=in_recv.at[number, k],
                device_id=(peer, ch),
                device_id_type=MESH,
            )
            copy.start()
            inbound[number].append(copy)
    for source, target in pieces:
        target[my_rows, :] = source[:, my_cols]
    filt_in[pl.ds(me, 1)] = filt_ref[my_groups, :].reshape(1, groups, filt_ref.shape[1])

    def send_back(source, target, number):
        copies = []
        for k in range(1, count_ctx):
            peer = lax.rem(me + k, count_ctx)
            peer_rows = pl.ds(pl.multiple_of(peer * rows, 16), rows)
            copy = pltpu.make_async_remote_copy(
                src_ref=source.at[peer_rows, :],
                dst_ref=target.at[:, my_cols],
                send_sem=back_send.at[number, k],
                recv_sem=back_recv.at[number, k],
                device_id=(peer, ch),
                device_id_type=MESH,
            )
            copy.start()
            copies.append(copy)
        target[:, my_cols] = source[my_rows, :]
        return copies

    for copy in inbound[4]:
        copy.wait_recv()
    fpad[...] = jnp.zeros_like(fpad)
    wide = filt_ref.shape[1]
    for j in range(count_ctx):
        first = HALF + j * rows
        base = first // HALF * HALF
        piece = jnp.concatenate(
            [filt_in[j], jnp.zeros((groups, HALF), jnp.float32)], axis=1
        )
        if first % HALF:
            piece = pltpu.roll(piece, first % HALF, 1)
        fpad[:, base : base + wide + HALF] += piece

    for copy in inbound[0]:
        copy.wait_recv()
    for j in range(tiles):
        turned = (
            gated_in[j * TILE : (j + 1) * TILE, :].astype(jnp.float32).T.astype(jnp.bfloat16)
        )
        for g in range(groups):
            x_turned[g, j * GROUP : (j + 1) * GROUP, :] = turned[g * GROUP : (g + 1) * GROUP, :]

    span = tokens + HALF

    def one_group(g, carry):
        line = fpad[pl.ds(g, 1), 0 : span + HALF]
        shifted = pltpu.roll(
            jnp.broadcast_to(line, (HALF, span + HALF)), 0, 1, stride=1, stride_axis=0
        ).astype(jnp.bfloat16)
        for d in range(tiles):
            block = jnp.concatenate(
                [
                    shifted[:, HALF + d * TILE : HALF + (d + 1) * TILE],
                    shifted[:, d * TILE : (d + 1) * TILE],
                ],
                axis=0,
            )
            part = jnp.dot(
                x_turned[g, 0 : (tiles - d) * GROUP, :], block, preferred_element_type=jnp.float32
            )
            if d == 0:
                y_turned[g] = part
            else:
                y_turned[g, d * GROUP :, :] += part
        return carry

    lax.fori_loop(0, groups, one_group, 0)
    for i in range(tiles):
        gathered = y_turned[:, i * GROUP : (i + 1) * GROUP, :].reshape(HD, TILE)
        conv_out[i * TILE : (i + 1) * TILE, :] = gathered.T.astype(jnp.bfloat16)
    conv_copies = send_back(conv_out, conv_back, 0)

    for number in (1, 2, 3):
        for copy in inbound[number]:
            copy.wait_recv()
    factor = HD ** (-0.5) * math.log2(math.e)
    below = lax.broadcasted_iota(jnp.int32, (TILE, TILE), 1) <= lax.broadcasted_iota(
        jnp.int32, (TILE, TILE), 0
    )
    for i in range(tiles):
        query = q_in[i * TILE : (i + 1) * TILE, :]
        scores = lax.dot_general(
            query,
            k_in[0 : (i + 1) * TILE, :],
            (((1,), (1,)), ((), ())),
            preferred_element_type=jnp.float32,
        )
        corner = jnp.where(below, scores[:, i * TILE :], neg_large)
        if i:
            scores = jnp.concatenate([scores[:, : i * TILE], corner], axis=1)
        else:
            scores = corner
        row_max = jnp.max(scores, axis=1, keepdims=True)
        weights = jnp.exp2((scores - row_max) * factor)
        totals = jnp.sum(weights, axis=1, keepdims=True)
        summed = jnp.dot(
            weights.astype(jnp.bfloat16),
            v_in[0 : (i + 1) * TILE, :],
            preferred_element_type=jnp.float32,
        )
        attn_out[i * TILE : (i + 1) * TILE, :] = (summed / totals).astype(jnp.bfloat16)
    attn_copies = send_back(attn_out, attn_back, 1)

    share = rows // 4
    padded = keep.shape[1] // 2
    order = (ch, pair_peer, core_peer, (1 - pair) * 2 + (1 - core))

    def place(target):
        for slot, owner in enumerate(order):
            part = stage[pl.ds(pl.multiple_of(owner * share, 8), share), :]
            filler = jnp.zeros((padded - share, width), jnp.float32)
            target[slot * padded : (slot + 1) * padded, :] = jnp.concatenate(
                [part, filler], axis=0
            ).astype(jnp.bfloat16)

    for copy in conv_copies:
        copy.wait_recv()
    stage[...] = qc_ref[...].astype(jnp.float32) * conv_back[...].astype(jnp.float32)
    place(lhs_conv)
    w1_copy.wait()
    w2_copy.wait()
    for copy in attn_copies:
        copy.wait_recv()
    stage[...] = attn_back[...].astype(jnp.float32)
    place(lhs_attn)

    chunks, unused, chunk = keep.shape

    def copy_a(n):
        return pltpu.make_async_remote_copy(
            src_ref=send_a.at[n],
            dst_ref=recv_a.at[n],
            send_sem=a_send.at[n],
            recv_sem=a_recv.at[n],
            device_id=(me, core_peer),
            device_id_type=MESH,
        )

    def copy_b(n):
        return pltpu.make_async_remote_copy(
            src_ref=send_b.at[n],
            dst_ref=recv_b.at[n],
            send_sem=b_send.at[n],
            recv_sem=b_recv.at[n],
            device_id=(me, pair_peer),
            device_id_type=MESH,
        )

    def project(n):
        cols = pl.ds(pl.multiple_of(n * chunk, chunk), chunk)
        total = jnp.dot(
            lhs_conv[...], w1[:, cols], preferred_element_type=jnp.float32
        ) + jnp.dot(lhs_attn[...], w2[:, cols], preferred_element_type=jnp.float32)
        keep[n] = total[0 : 2 * padded]
        send_a[n] = total[2 * padded :].astype(jnp.bfloat16)
        copy_a(n).start()

    def forward(n):
        copy_a(n).wait_recv()
        send_b[n] = (
            keep[n, padded:, :] + recv_a[n, padded:, :].astype(jnp.float32)
        ).astype(jnp.bfloat16)
        copy_b(n).start()

    project(0)

    def one_chunk(n, carry):
        project(n)
        forward(n - 1)
        return carry

    lax.fori_loop(1, chunks, one_chunk, 0)
    forward(chunks - 1)

    def finish(n, carry):
        cols = pl.ds(pl.multiple_of(n * chunk, chunk), chunk)
        copy_b(n).wait_recv()
        total = (
            keep[n, 0:padded, :]
            + recv_a[n, 0:padded, :].astype(jnp.float32)
            + recv_b[n].astype(jnp.float32)
        )
        out_ref[:, cols] = total[0:share].astype(jnp.bfloat16)
        copy_a(n).wait_send()
        copy_b(n).wait_send()
        return carry

    lax.fori_loop(0, chunks, finish, 0)
    for copies in inbound + [conv_copies, attn_copies]:
        for copy in copies:
            copy.wait_send()


def local_fused(q_conv, k_conv, v_conv, conv_filter, q_attn, k_attn, v_attn, w_conv_out, w_attn_out):
    count_ctx = lax.axis_size("ctx")
    rows, width = q_conv.shape
    dout = w_conv_out.shape[1]
    tokens = count_ctx * rows
    groups = HD // GROUP
    wide = (rows + HALF - 1) // HALF * HALF
    filt = jnp.pad(conv_filter.T.astype(jnp.float32), ((0, 0), (0, wide - rows)))
    share = rows // 4
    padded = (share + 15) // 16 * 16
    chunk = 512
    chunks = dout // chunk
    tiles = tokens // TILE
    bf16, f32 = jnp.bfloat16, jnp.float32
    vmem = pl.BlockSpec(memory_space=pltpu.VMEM)
    hbm = pl.BlockSpec(memory_space=pl.ANY)
    dma = pltpu.SemaphoreType.DMA
    return pl.pallas_call(
        partial(fused_kernel, count_ctx, rows, width),
        out_shape=jax.ShapeDtypeStruct((share, dout), bf16),
        in_specs=[vmem] * 7 + [hbm] * 2,
        out_specs=vmem,
        scratch_shapes=[
            pltpu.VMEM((rows, width), bf16),
            pltpu.VMEM((count_ctx, groups, wide), f32),
            pltpu.VMEM((tokens, HD), bf16),
            pltpu.VMEM((tokens, HD), bf16),
            pltpu.VMEM((tokens, HD), bf16),
            pltpu.VMEM((tokens, HD), bf16),
            pltpu.VMEM((tokens, HD), bf16),
            pltpu.VMEM((tokens, HD), bf16),
            pltpu.VMEM((rows, width), bf16),
            pltpu.VMEM((rows, width), bf16),
            pltpu.VMEM((groups, tokens + 2 * HALF + TILE), f32),
            pltpu.VMEM((groups, tiles * GROUP, TILE), bf16),
            pltpu.VMEM((groups, tiles * GROUP, TILE), f32),
            pltpu.VMEM((rows, width), f32),
            pltpu.VMEM((4 * padded, width), bf16),
            pltpu.VMEM((4 * padded, width), bf16),
            pltpu.VMEM(w_conv_out.shape, bf16),
            pltpu.VMEM(w_attn_out.shape, bf16),
            pltpu.VMEM((chunks, 2 * padded, chunk), f32),
            pltpu.VMEM((chunks, 2 * padded, chunk), bf16),
            pltpu.VMEM((chunks, 2 * padded, chunk), bf16),
            pltpu.VMEM((chunks, padded, chunk), bf16),
            pltpu.VMEM((chunks, padded, chunk), bf16),
            dma((5, count_ctx)),
            dma((5, count_ctx)),
            dma((2, count_ctx)),
            dma((2, count_ctx)),
            dma((2,)),
            dma((chunks,)),
            dma((chunks,)),
            dma((chunks,)),
            dma((chunks,)),
        ],
        compiler_params=pltpu.CompilerParams(
            collective_id=0, has_side_effects=True, vmem_limit_bytes=56 * 1024 * 1024
        ),
        name="fused_block",
    )(q_conv, k_conv, v_conv, filt, q_attn, k_attn, v_attn, w_conv_out, w_attn_out)


def local(q_conv, k_conv, v_conv, conv_filter, q_attn, k_attn, v_attn, w_conv_out, w_attn_out):
    count_ctx = lax.axis_size("ctx")
    rows, width = q_conv.shape
    dout = w_conv_out.shape[1]
    fits = (
        width == count_ctx * HD
        and conv_filter.shape[1] * GROUP == width
        and lax.axis_size("ch") == 4
        and rows % 32 == 0
        and (count_ctx * rows) % TILE == 0
        and count_ctx * rows <= 2048
        and dout % 512 == 0
    )
    chosen = local_fused if fits else local_general
    return chosen(
        q_conv, k_conv, v_conv, conv_filter, q_attn, k_attn, v_attn, w_conv_out, w_attn_out
    )


def solution(mesh):
    return jax.shard_map(
        local,
        mesh=mesh,
        in_specs=(
            P("ctx", "ch"),
            P("ctx", "ch"),
            P("ctx", "ch"),
            P("ctx", "ch"),
            P("ctx", "ch"),
            P("ctx", "ch"),
            P("ctx", "ch"),
            P("ch", None),
            P("ch", None),
        ),
        out_specs=P(("ctx", "ch"), None),
        check_vma=False,
    )
```

```python
from functools import partial
import math

import jax
import jax.numpy as jnp
from jax import lax
from jax.experimental import pallas as pl
from jax.experimental.pallas import tpu as pltpu
from jax.sharding import PartitionSpec as P

HD = 128


two_pi = 2.0 * math.pi
neg_large = -1e30
highest = lax.Precision.HIGHEST


def angle_table(left_idx, right_idx, period):
    product = left_idx[:, None] * right_idx[None, :] % period
    return product.astype(jnp.float32) * (two_pi / period)


def section_coarse(values, cos_table, sin_table, twiddle):
    real_part = jnp.einsum("kn,nsc->ksc", cos_table, values, precision=highest)
    imag_part = -jnp.einsum("kn,nsc->ksc", sin_table, values, precision=highest)
    cos_twist = jnp.cos(twiddle)[:, :, None]
    sin_twist = jnp.sin(twiddle)[:, :, None]
    return (
        real_part * cos_twist + imag_part * sin_twist,
        imag_part * cos_twist - real_part * sin_twist,
    )


def section_fine(real_part, imag_part, cos_table, sin_table, direction):
    cos_real = jnp.einsum("kn,anc->akc", cos_table, real_part, precision=highest)
    cos_imag = jnp.einsum("kn,anc->akc", cos_table, imag_part, precision=highest)
    sin_real = jnp.einsum("kn,anc->akc", sin_table, real_part, precision=highest)
    sin_imag = jnp.einsum("kn,anc->akc", sin_table, imag_part, precision=highest)
    return (cos_real - direction * sin_imag, cos_imag + direction * sin_real)


def spectral_conv(gated, filters, my_index, tok_rows, count_ctx):
    chans = gated.shape[1]
    groups = filters.shape[1]
    share = chans // groups
    sub_rows = tok_rows // count_ctx
    period = 2 * count_ctx * tok_rows
    got_source, got_filter = (
        lax.all_to_all(
            gated.reshape(1, tok_rows, chans), "ctx", split_axis=1, concat_axis=0, tiled=True
        ),
        lax.all_to_all(
            filters.reshape(1, tok_rows, groups), "ctx", split_axis=1, concat_axis=0, tiled=True
        ),
    )
    coarse_idx = jnp.arange(count_ctx, dtype=jnp.int32)
    coarse_freq = jnp.arange(2 * count_ctx, dtype=jnp.int32)
    coarse_angle = angle_table(coarse_freq, coarse_idx, 2 * count_ctx)
    cos_coarse = jnp.cos(coarse_angle)
    sin_coarse = jnp.sin(coarse_angle)
    fine_global = my_index * sub_rows + jnp.arange(sub_rows, dtype=jnp.int32)
    twist_in = angle_table(coarse_freq, fine_global, period)
    source_re, source_im = section_coarse(
        got_source.astype(jnp.float32), cos_coarse, sin_coarse, twist_in
    )
    filter_re, filter_im = section_coarse(
        got_filter.astype(jnp.float32), cos_coarse, sin_coarse, twist_in
    )
    source_re, source_im, filter_re, filter_im = (
        lax.all_to_all(
            source_re.astype(jnp.bfloat16), "ctx", split_axis=0, concat_axis=1, tiled=True
        ).astype(source_re.dtype),
        lax.all_to_all(
            source_im.astype(jnp.bfloat16), "ctx", split_axis=0, concat_axis=1, tiled=True
        ).astype(source_im.dtype),
        lax.all_to_all(
            filter_re.astype(jnp.bfloat16), "ctx", split_axis=0, concat_axis=1, tiled=True
        ).astype(filter_re.dtype),
        lax.all_to_all(
            filter_im.astype(jnp.bfloat16), "ctx", split_axis=0, concat_axis=1, tiled=True
        ).astype(filter_im.dtype),
    )
    fine_idx = jnp.arange(tok_rows, dtype=jnp.int32)
    fine_angle = angle_table(fine_idx, fine_idx, tok_rows)
    cos_fine = jnp.cos(fine_angle)
    sin_fine = jnp.sin(fine_angle)
    source_re, source_im = section_fine(source_re, source_im, cos_fine, sin_fine, -1.0)
    filter_re, filter_im = section_fine(filter_re, filter_im, cos_fine, sin_fine, -1.0)
    split_re = source_re.reshape(2, tok_rows, groups, share)
    split_im = source_im.reshape(2, tok_rows, groups, share)
    prod_re = split_re * filter_re[..., None] - split_im * filter_im[..., None]
    prod_im = split_re * filter_im[..., None] + split_im * filter_re[..., None]
    back_re, back_im = section_fine(
        prod_re.reshape(2, tok_rows, chans),
        prod_im.reshape(2, tok_rows, chans),
        cos_fine,
        sin_fine,
        1.0,
    )
    pair_freq = my_index * 2 + jnp.arange(2, dtype=jnp.int32)
    twist_out = angle_table(pair_freq, fine_idx, period)
    cos_out = jnp.cos(twist_out)[:, :, None]
    sin_out = jnp.sin(twist_out)[:, :, None]
    turned_re = back_re * cos_out - back_im * sin_out
    turned_im = back_re * sin_out + back_im * cos_out
    turned_re, turned_im = (
        lax.all_to_all(
            turned_re.astype(jnp.bfloat16), "ctx", split_axis=1, concat_axis=0, tiled=True
        ).astype(turned_re.dtype),
        lax.all_to_all(
            turned_im.astype(jnp.bfloat16), "ctx", split_axis=1, concat_axis=0, tiled=True
        ).astype(turned_im.dtype),
    )
    result = jnp.einsum("nk,ksc->nsc", cos_coarse.T, turned_re, precision=highest)
    result = result - jnp.einsum("nk,ksc->nsc", sin_coarse.T, turned_im, precision=highest)
    rounded = (result / period).astype(jnp.bfloat16)
    returned = lax.all_to_all(rounded, "ctx", split_axis=0, concat_axis=1, tiled=True)
    return returned.reshape(tok_rows, chans)


def keep_same(running):
    return running


def attend_block(group_query, group_pos, key_block, value_block, key_pos, score_scale, group_state):
    run_max, run_total, run_accum = group_state
    scores = (
        jnp.einsum("thd,shd->hts", group_query, key_block, preferred_element_type=jnp.float32)
        * score_scale
    )
    allowed = (key_pos[None, :] <= group_pos[:, None])[None]
    block_max = jnp.max(jnp.where(allowed, scores, neg_large), axis=2)
    new_max = jnp.maximum(run_max, block_max)
    factor = jnp.exp(run_max - new_max)
    weights = jnp.where(allowed, jnp.exp(scores - new_max[:, :, None]), 0.0)
    new_total = run_total * factor + jnp.sum(weights, axis=2)
    new_accum = run_accum * factor[:, :, None] + jnp.einsum(
        "hts,shd->htd",
        weights.astype(jnp.bfloat16),
        value_block,
        preferred_element_type=jnp.float32,
    )
    return (new_max, new_total, new_accum)


def attention(q_attn, k_attn, v_attn, my_index, tok_rows):
    heads_local = q_attn.shape[1] // HD
    score_scale = HD ** (-0.5)
    queries = q_attn.reshape(tok_rows, heads_local, HD)
    group_list = [(queries, my_index * tok_rows + jnp.arange(tok_rows, dtype=jnp.int32))]
    initial = tuple(
        (
            (
                jnp.full((heads_local, entry[0].shape[0]), neg_large, jnp.float32),
                jnp.zeros((heads_local, entry[0].shape[0]), jnp.float32),
                jnp.zeros((heads_local, entry[0].shape[0], HD), jnp.float32),
            )
            for entry in group_list
        )
    )
    key_piece = lax.all_gather(k_attn, "ctx", axis=0, tiled=True)
    value_piece = lax.all_gather(v_attn, "ctx", axis=0, tiled=True)
    count_blocks = key_piece.shape[0] // tok_rows
    keys_split = key_piece.reshape(count_blocks, tok_rows, heads_local, HD)
    values_split = value_piece.reshape(count_blocks, tok_rows, heads_local, HD)

    def one_block(carry, item):
        key_block, value_block, block_number = item
        block_first = block_number * tok_rows
        key_pos = block_first + jnp.arange(tok_rows, dtype=jnp.int32)
        updated = []
        for entry, group_state in zip(group_list, carry):
            step_fn = partial(
                attend_block, entry[0], entry[1], key_block, value_block, key_pos, score_scale
            )
            updated.append(lax.cond(block_first <= entry[1][-1], step_fn, keep_same, group_state))
        return (tuple(updated), None)

    new_state, unused = lax.scan(
        one_block, initial, (keys_split, values_split, jnp.arange(count_blocks, dtype=jnp.int32))
    )
    outputs = [
        (state[2] / state[1][:, :, None]).transpose(1, 0, 2).astype(jnp.bfloat16)
        for state in new_state
    ]
    merged = outputs[0]
    return merged.reshape(tok_rows, heads_local * HD)


def local_general(q_conv, k_conv, v_conv, conv_filter, q_attn, k_attn, v_attn, w_conv_out, w_attn_out):
    count_ctx = lax.axis_size("ctx")
    my_index = lax.axis_index("ctx")
    tok_rows = q_conv.shape[0]
    gated = (k_conv.astype(jnp.float32) * v_conv.astype(jnp.float32)).astype(jnp.bfloat16)
    conv = spectral_conv(gated, conv_filter, my_index, tok_rows, count_ctx)
    mixed = (q_conv.astype(jnp.float32) * conv.astype(jnp.float32)).astype(jnp.bfloat16)
    attended = attention(q_attn, k_attn, v_attn, my_index, tok_rows)
    return lax.psum_scatter(
        (
            jnp.dot(mixed, w_conv_out, preferred_element_type=jnp.float32)
            + jnp.dot(attended, w_attn_out, preferred_element_type=jnp.float32)
        ).astype(jnp.bfloat16),
        "ch",
        scatter_dimension=0,
        tiled=True,
    )


GROUP = 16
TILE = 256
HALF = 128
MESH = pl.DeviceIdType.MESH


def fused_kernel(
    count_ctx, rows, width,
    qc_hbm, kc_hbm, vc_hbm, filt_ref, q_ref, k_ref, v_ref, w1_hbm, w2_hbm,
    out_ref,
    qc, kc, vc, filt,
    gated, filt_in, gated_in, q_in, k_in, v_in, conv_out, attn_out, conv_back, attn_back,
    fpad, x_turned, y_turned, stage, lhs_conv, lhs_attn, w1, w2,
    keep, send_a, recv_a, send_b, recv_b,
    in_send, in_recv, back_send, back_recv, load_sem, a_send, a_recv, b_send, b_recv,
):
    me = lax.axis_index("ctx")
    ch = lax.axis_index("ch")
    core = lax.rem(ch, 2)
    pair = ch // 2
    core_peer = pair * 2 + (1 - core)
    pair_peer = (1 - pair) * 2 + core
    tokens = count_ctx * rows
    tiles = tokens // TILE
    groups = HD // GROUP
    my_rows = pl.ds(pl.multiple_of(me * rows, 16), rows)
    my_cols = pl.ds(pl.multiple_of(me * HD, HD), HD)
    my_groups = pl.ds(pl.multiple_of(me * groups, groups), groups)

    barrier = pltpu.get_barrier_semaphore()
    for k in range(1, count_ctx):
        peer = lax.rem(me + k, count_ctx)
        pl.semaphore_signal(barrier, inc=1, device_id=(peer, ch), device_id_type=MESH)
    pl.semaphore_signal(barrier, inc=1, device_id=(me, core_peer), device_id_type=MESH)
    pl.semaphore_signal(barrier, inc=1, device_id=(me, pair_peer), device_id_type=MESH)

    heads = ((q_ref, q_in), (k_ref, k_in), (v_ref, v_in))
    kc_copy = pltpu.make_async_copy(kc_hbm, kc, load_sem.at[0])
    vc_copy = pltpu.make_async_copy(vc_hbm, vc, load_sem.at[1])
    own_copies = [
        pltpu.make_async_copy(source.at[:, my_cols], target.at[my_rows, :], load_sem.at[2 + n])
        for n, (source, target) in enumerate(heads)
    ]
    qc_copy = pltpu.make_async_copy(qc_hbm, qc, load_sem.at[5])
    w1_copy = pltpu.make_async_copy(w1_hbm, w1, load_sem.at[6])
    w2_copy = pltpu.make_async_copy(w2_hbm, w2, load_sem.at[7])
    kc_copy.start()
    vc_copy.start()
    filt[...] = jnp.zeros_like(filt)
    filt[:, 0:rows] = filt_ref[...].astype(jnp.float32)
    pl.semaphore_wait(barrier, count_ctx + 1)

    inbound = [[] for unused in range(5)]

    def spread(source, target, number):
        for k in range(1, count_ctx):
            peer = lax.rem(me + k, count_ctx)
            peer_cols = pl.ds(pl.multiple_of(peer * HD, HD), HD)
            copy = pltpu.make_async_remote_copy(
                src_ref=source.at[:, peer_cols],
                dst_ref=target.at[my_rows, :],
                send_sem=in_send.at[number, k],
                recv_sem=in_recv.at[number, k],
                device_id=(peer, ch),
                device_id_type=MESH,
            )
            copy.start()
            inbound[number].append(copy)

    for k in range(1, count_ctx):
        peer = lax.rem(me + k, count_ctx)
        peer_groups = pl.ds(pl.multiple_of(peer * groups, groups), groups)
        copy = pltpu.make_async_remote_copy(
            src_ref=filt.at[peer_groups, :],
            dst_ref=filt_in.at[me],
            send_sem=in_send.at[4, k],
            recv_sem=in_recv.at[4, k],
            device_id=(peer, ch),
            device_id_type=MESH,
        )
        copy.start()
        inbound[4].append(copy)
    for number, (source, target) in enumerate(heads):
        spread(source, target, number + 1)
    for copy in own_copies + [qc_copy, w1_copy, w2_copy]:
        copy.start()
    kc_copy.wait()
    vc_copy.wait()
    gated[...] = (kc[...].astype(jnp.float32) * vc[...].astype(jnp.float32)).astype(jnp.bfloat16)
    spread(gated, gated_in, 0)
    gated_in[my_rows, :] = gated[:, my_cols]
    filt_in[pl.ds(me, 1)] = filt[my_groups, :].reshape(1, groups, filt.shape[1])

    def send_back(source, target, number, first, count):
        copies = []
        here = pl.ds(pl.multiple_of(first, 16), count)
        for k in range(1, count_ctx):
            peer = lax.rem(me + k, count_ctx)
            peer_rows = pl.ds(pl.multiple_of(peer * rows + first, 16), count)
            copy = pltpu.make_async_remote_copy(
                src_ref=source.at[peer_rows, :],
                dst_ref=target.at[here, my_cols],
                send_sem=back_send.at[number, k],
                recv_sem=back_recv.at[number, k],
                device_id=(peer, ch),
                device_id_type=MESH,
            )
            copy.start()
            copies.append(copy)
        kept_rows = pl.ds(pl.multiple_of(me * rows + first, 16), count)
        target[here, my_cols] = source[kept_rows, :]
        return copies

    for copy in own_copies:
        copy.wait()
    for number in (1, 2, 3):
        for copy in inbound[number]:
            copy.wait_recv()
    factor = HD ** (-0.5) * math.log2(math.e)
    below = lax.broadcasted_iota(jnp.int32, (TILE, TILE), 1) <= lax.broadcasted_iota(
        jnp.int32, (TILE, TILE), 0
    )
    for i in range(tiles):
        query = q_in[i * TILE : (i + 1) * TILE, :]
        scores = lax.dot_general(
            query,
            k_in[0 : (i + 1) * TILE, :],
            (((1,), (1,)), ((), ())),
            preferred_element_type=jnp.float32,
        )
        corner = jnp.where(below, scores[:, i * TILE :], neg_large)
        if i:
            scores = jnp.concatenate([scores[:, : i * TILE], corner], axis=1)
        else:
            scores = corner
        row_max = jnp.max(scores, axis=1, keepdims=True)
        weights = jnp.exp2((scores - row_max) * factor)
        totals = jnp.sum(weights, axis=1, keepdims=True)
        summed = jnp.dot(
            weights.astype(jnp.bfloat16),
            v_in[0 : (i + 1) * TILE, :],
            preferred_element_type=jnp.float32,
        )
        attn_out[i * TILE : (i + 1) * TILE, :] = (summed / totals).astype(jnp.bfloat16)
    attn_copies = send_back(attn_out, attn_back, 0, 0, rows)

    for copy in inbound[4]:
        copy.wait_recv()
    fpad[...] = jnp.zeros_like(fpad)
    wide = filt.shape[1]
    for j in range(count_ctx):
        first = HALF + j * rows
        base = first // HALF * HALF
        piece = jnp.concatenate(
            [filt_in[j], jnp.zeros((groups, HALF), jnp.float32)], axis=1
        )
        if first % HALF:
            piece = pltpu.roll(piece, first % HALF, 1)
        fpad[:, base : base + wide + HALF] += piece

    for copy in inbound[0]:
        copy.wait_recv()
    for j in range(tiles):
        turned = (
            gated_in[j * TILE : (j + 1) * TILE, :].astype(jnp.float32).T.astype(jnp.bfloat16)
        )
        for g in range(groups):
            x_turned[g, j * GROUP : (j + 1) * GROUP, :] = turned[g * GROUP : (g + 1) * GROUP, :]

    span = tokens + HALF

    def one_group(g, carry):
        line = fpad[pl.ds(g, 1), 0 : span + HALF]
        shifted = pltpu.roll(
            jnp.broadcast_to(line, (HALF, span + HALF)), 0, 1, stride=1, stride_axis=0
        ).astype(jnp.bfloat16)
        for d in range(tiles):
            block = jnp.concatenate(
                [
                    shifted[:, HALF + d * TILE : HALF + (d + 1) * TILE],
                    shifted[:, d * TILE : (d + 1) * TILE],
                ],
                axis=0,
            )
            part = jnp.dot(
                x_turned[g, 0 : (tiles - d) * GROUP, :], block, preferred_element_type=jnp.float32
            )
            if d == 0:
                y_turned[g] = part
            else:
                y_turned[g, d * GROUP :, :] += part
        return carry

    lax.fori_loop(0, groups, one_group, 0)
    for i in range(tiles):
        gathered = y_turned[:, i * GROUP : (i + 1) * GROUP, :].reshape(HD, TILE)
        conv_out[i * TILE : (i + 1) * TILE, :] = gathered.T.astype(jnp.bfloat16)
    half = rows // 2
    halves = (half * (1 - pair), half * pair)
    conv_copies = [
        send_back(conv_out, conv_back, 1 + n, first, half) for n, first in enumerate(halves)
    ]

    share = rows // 4
    padded = keep.shape[1]
    chunk = keep.shape[2]
    chunks = keep.shape[0] // 2

    def place(target):
        for slot, owner in enumerate((core, 1 - core)):
            part = stage[pl.ds(pl.multiple_of(owner * share, 8), share), :]
            filler = jnp.zeros((padded - share, width), jnp.float32)
            target[slot * padded : (slot + 1) * padded, :] = jnp.concatenate(
                [part, filler], axis=0
            ).astype(jnp.bfloat16)

    def take(first):
        here = pl.ds(pl.multiple_of(first, 16), half)
        stage[...] = qc[here, :].astype(jnp.float32) * conv_back[here, :].astype(jnp.float32)
        place(lhs_conv)
        stage[...] = attn_back[here, :].astype(jnp.float32)
        place(lhs_attn)

    def copy_a(n):
        return pltpu.make_async_remote_copy(
            src_ref=send_a.at[n],
            dst_ref=recv_a.at[n],
            send_sem=a_send.at[n],
            recv_sem=a_recv.at[n],
            device_id=(me, core_peer),
            device_id_type=MESH,
        )

    def copy_b(n):
        return pltpu.make_async_remote_copy(
            src_ref=send_b.at[n],
            dst_ref=recv_b.at[n],
            send_sem=b_send.at[n],
            recv_sem=b_recv.at[n],
            device_id=(me, pair_peer),
            device_id_type=MESH,
        )

    def project(n, base):
        cols = pl.ds(pl.multiple_of(n * chunk, chunk), chunk)
        total = jnp.dot(
            lhs_conv[...], w1[:, cols], preferred_element_type=jnp.float32
        ) + jnp.dot(lhs_attn[...], w2[:, cols], preferred_element_type=jnp.float32)
        keep[base + n] = total[0:padded]
        send_a[base + n] = total[padded:].astype(jnp.bfloat16)
        copy_a(base + n).start()

    def forward(n):
        copy_a(n).wait_recv()
        send_b[n] = (keep[n] + recv_a[n].astype(jnp.float32)).astype(jnp.bfloat16)
        copy_b(n).start()

    for copy in (qc_copy, w1_copy, w2_copy):
        copy.wait()
    for copy in attn_copies + conv_copies[0]:
        copy.wait_recv()
    take(halves[0])
    project(0, 0)

    def first_half(n, carry):
        project(n, 0)
        forward(n - 1)
        return carry

    lax.fori_loop(1, chunks, first_half, 0)
    forward(chunks - 1)
    for copy in conv_copies[1]:
        copy.wait_recv()
    take(halves[1])

    def second_half(n, carry):
        project(n, chunks)
        return carry

    lax.fori_loop(0, chunks, second_half, 0)

    def finish(n, carry):
        cols = pl.ds(pl.multiple_of(n * chunk, chunk), chunk)
        copy_a(chunks + n).wait_recv()
        copy_b(n).wait_recv()
        total = (
            keep[chunks + n]
            + recv_a[chunks + n].astype(jnp.float32)
            + recv_b[n].astype(jnp.float32)
        )
        out_ref[:, cols] = total[0:share].astype(jnp.bfloat16)
        copy_a(n).wait_send()
        copy_a(chunks + n).wait_send()
        copy_b(n).wait_send()
        return carry

    lax.fori_loop(0, chunks, finish, 0)
    for copies in inbound + conv_copies + [attn_copies]:
        for copy in copies:
            copy.wait_send()


def local_fused(q_conv, k_conv, v_conv, conv_filter, q_attn, k_attn, v_attn, w_conv_out, w_attn_out):
    count_ctx = lax.axis_size("ctx")
    rows, width = q_conv.shape
    dout = w_conv_out.shape[1]
    tokens = count_ctx * rows
    groups = HD // GROUP
    wide = (rows + HALF - 1) // HALF * HALF
    share = rows // 4
    padded = (share + 15) // 16 * 16
    chunk = 512
    chunks = dout // chunk
    tiles = tokens // TILE
    bf16, f32 = jnp.bfloat16, jnp.float32
    vmem = pl.BlockSpec(memory_space=pltpu.VMEM)
    hbm = pl.BlockSpec(memory_space=pl.ANY)
    dma = pltpu.SemaphoreType.DMA
    return pl.pallas_call(
        partial(fused_kernel, count_ctx, rows, width),
        out_shape=jax.ShapeDtypeStruct((share, dout), bf16),
        in_specs=[hbm] * 3 + [vmem] + [hbm] * 5,
        out_specs=vmem,
        scratch_shapes=[
            pltpu.VMEM((rows, width), bf16),
            pltpu.VMEM((rows, width), bf16),
            pltpu.VMEM((rows, width), bf16),
            pltpu.VMEM((conv_filter.shape[1], wide), f32),
            pltpu.VMEM((rows, width), bf16),
            pltpu.VMEM((count_ctx, groups, wide), f32),
            pltpu.VMEM((tokens, HD), bf16),
            pltpu.VMEM((tokens, HD), bf16),
            pltpu.VMEM((tokens, HD), bf16),
            pltpu.VMEM((tokens, HD), bf16),
            pltpu.VMEM((tokens, HD), bf16),
            pltpu.VMEM((tokens, HD), bf16),
            pltpu.VMEM((rows, width), bf16),
            pltpu.VMEM((rows, width), bf16),
            pltpu.VMEM((groups, tokens + 2 * HALF + TILE), f32),
            pltpu.VMEM((groups, tiles * GROUP, TILE), bf16),
            pltpu.VMEM((groups, tiles * GROUP, TILE), f32),
            pltpu.VMEM((rows // 2, width), f32),
            pltpu.VMEM((2 * padded, width), bf16),
            pltpu.VMEM((2 * padded, width), bf16),
            pltpu.VMEM(w_conv_out.shape, bf16),
            pltpu.VMEM(w_attn_out.shape, bf16),
            pltpu.VMEM((2 * chunks, padded, chunk), f32),
            pltpu.VMEM((2 * chunks, padded, chunk), bf16),
            pltpu.VMEM((2 * chunks, padded, chunk), bf16),
            pltpu.VMEM((chunks, padded, chunk), bf16),
            pltpu.VMEM((chunks, padded, chunk), bf16),
            dma((5, count_ctx)),
            dma((5, count_ctx)),
            dma((3, count_ctx)),
            dma((3, count_ctx)),
            dma((8,)),
            dma((2 * chunks,)),
            dma((2 * chunks,)),
            dma((chunks,)),
            dma((chunks,)),
        ],
        compiler_params=pltpu.CompilerParams(
            collective_id=0, has_side_effects=True, vmem_limit_bytes=56 * 1024 * 1024
        ),
        name="fused_block",
    )(q_conv, k_conv, v_conv, conv_filter.T, q_attn, k_attn, v_attn, w_conv_out, w_attn_out)


def local(q_conv, k_conv, v_conv, conv_filter, q_attn, k_attn, v_attn, w_conv_out, w_attn_out):
    count_ctx = lax.axis_size("ctx")
    rows, width = q_conv.shape
    dout = w_conv_out.shape[1]
    fits = (
        width == count_ctx * HD
        and conv_filter.shape[1] * GROUP == width
        and lax.axis_size("ch") == 4
        and rows % 32 == 0
        and (count_ctx * rows) % TILE == 0
        and count_ctx * rows <= 2048
        and dout % 512 == 0
    )
    chosen = local_fused if fits else local_general
    return chosen(
        q_conv, k_conv, v_conv, conv_filter, q_attn, k_attn, v_attn, w_conv_out, w_attn_out
    )


def solution(mesh):
    return jax.shard_map(
        local,
        mesh=mesh,
        in_specs=(
            P("ctx", "ch"),
            P("ctx", "ch"),
            P("ctx", "ch"),
            P("ctx", "ch"),
            P("ctx", "ch"),
            P("ctx", "ch"),
            P("ctx", "ch"),
            P("ch", None),
            P("ch", None),
        ),
        out_specs=P(("ctx", "ch"), None),
        check_vma=False,
    )
```

```python
from functools import partial
import math

import jax
import jax.numpy as jnp
from jax import lax
from jax.experimental import pallas as pl
from jax.experimental.pallas import tpu as pltpu
from jax.sharding import PartitionSpec as P

HD = 128


two_pi = 2.0 * math.pi
neg_large = -1e30
highest = lax.Precision.HIGHEST


def angle_table(left_idx, right_idx, period):
    product = left_idx[:, None] * right_idx[None, :] % period
    return product.astype(jnp.float32) * (two_pi / period)


def section_coarse(values, cos_table, sin_table, twiddle):
    real_part = jnp.einsum("kn,nsc->ksc", cos_table, values, precision=highest)
    imag_part = -jnp.einsum("kn,nsc->ksc", sin_table, values, precision=highest)
    cos_twist = jnp.cos(twiddle)[:, :, None]
    sin_twist = jnp.sin(twiddle)[:, :, None]
    return (
        real_part * cos_twist + imag_part * sin_twist,
        imag_part * cos_twist - real_part * sin_twist,
    )


def section_fine(real_part, imag_part, cos_table, sin_table, direction):
    cos_real = jnp.einsum("kn,anc->akc", cos_table, real_part, precision=highest)
    cos_imag = jnp.einsum("kn,anc->akc", cos_table, imag_part, precision=highest)
    sin_real = jnp.einsum("kn,anc->akc", sin_table, real_part, precision=highest)
    sin_imag = jnp.einsum("kn,anc->akc", sin_table, imag_part, precision=highest)
    return (cos_real - direction * sin_imag, cos_imag + direction * sin_real)


def spectral_conv(gated, filters, my_index, tok_rows, count_ctx):
    chans = gated.shape[1]
    groups = filters.shape[1]
    share = chans // groups
    sub_rows = tok_rows // count_ctx
    period = 2 * count_ctx * tok_rows
    got_source, got_filter = (
        lax.all_to_all(
            gated.reshape(1, tok_rows, chans), "ctx", split_axis=1, concat_axis=0, tiled=True
        ),
        lax.all_to_all(
            filters.reshape(1, tok_rows, groups), "ctx", split_axis=1, concat_axis=0, tiled=True
        ),
    )
    coarse_idx = jnp.arange(count_ctx, dtype=jnp.int32)
    coarse_freq = jnp.arange(2 * count_ctx, dtype=jnp.int32)
    coarse_angle = angle_table(coarse_freq, coarse_idx, 2 * count_ctx)
    cos_coarse = jnp.cos(coarse_angle)
    sin_coarse = jnp.sin(coarse_angle)
    fine_global = my_index * sub_rows + jnp.arange(sub_rows, dtype=jnp.int32)
    twist_in = angle_table(coarse_freq, fine_global, period)
    source_re, source_im = section_coarse(
        got_source.astype(jnp.float32), cos_coarse, sin_coarse, twist_in
    )
    filter_re, filter_im = section_coarse(
        got_filter.astype(jnp.float32), cos_coarse, sin_coarse, twist_in
    )
    source_re, source_im, filter_re, filter_im = (
        lax.all_to_all(
            source_re.astype(jnp.bfloat16), "ctx", split_axis=0, concat_axis=1, tiled=True
        ).astype(source_re.dtype),
        lax.all_to_all(
            source_im.astype(jnp.bfloat16), "ctx", split_axis=0, concat_axis=1, tiled=True
        ).astype(source_im.dtype),
        lax.all_to_all(
            filter_re.astype(jnp.bfloat16), "ctx", split_axis=0, concat_axis=1, tiled=True
        ).astype(filter_re.dtype),
        lax.all_to_all(
            filter_im.astype(jnp.bfloat16), "ctx", split_axis=0, concat_axis=1, tiled=True
        ).astype(filter_im.dtype),
    )
    fine_idx = jnp.arange(tok_rows, dtype=jnp.int32)
    fine_angle = angle_table(fine_idx, fine_idx, tok_rows)
    cos_fine = jnp.cos(fine_angle)
    sin_fine = jnp.sin(fine_angle)
    source_re, source_im = section_fine(source_re, source_im, cos_fine, sin_fine, -1.0)
    filter_re, filter_im = section_fine(filter_re, filter_im, cos_fine, sin_fine, -1.0)
    split_re = source_re.reshape(2, tok_rows, groups, share)
    split_im = source_im.reshape(2, tok_rows, groups, share)
    prod_re = split_re * filter_re[..., None] - split_im * filter_im[..., None]
    prod_im = split_re * filter_im[..., None] + split_im * filter_re[..., None]
    back_re, back_im = section_fine(
        prod_re.reshape(2, tok_rows, chans),
        prod_im.reshape(2, tok_rows, chans),
        cos_fine,
        sin_fine,
        1.0,
    )
    pair_freq = my_index * 2 + jnp.arange(2, dtype=jnp.int32)
    twist_out = angle_table(pair_freq, fine_idx, period)
    cos_out = jnp.cos(twist_out)[:, :, None]
    sin_out = jnp.sin(twist_out)[:, :, None]
    turned_re = back_re * cos_out - back_im * sin_out
    turned_im = back_re * sin_out + back_im * cos_out
    turned_re, turned_im = (
        lax.all_to_all(
            turned_re.astype(jnp.bfloat16), "ctx", split_axis=1, concat_axis=0, tiled=True
        ).astype(turned_re.dtype),
        lax.all_to_all(
            turned_im.astype(jnp.bfloat16), "ctx", split_axis=1, concat_axis=0, tiled=True
        ).astype(turned_im.dtype),
    )
    result = jnp.einsum("nk,ksc->nsc", cos_coarse.T, turned_re, precision=highest)
    result = result - jnp.einsum("nk,ksc->nsc", sin_coarse.T, turned_im, precision=highest)
    rounded = (result / period).astype(jnp.bfloat16)
    returned = lax.all_to_all(rounded, "ctx", split_axis=0, concat_axis=1, tiled=True)
    return returned.reshape(tok_rows, chans)


def keep_same(running):
    return running


def attend_block(group_query, group_pos, key_block, value_block, key_pos, score_scale, group_state):
    run_max, run_total, run_accum = group_state
    scores = (
        jnp.einsum("thd,shd->hts", group_query, key_block, preferred_element_type=jnp.float32)
        * score_scale
    )
    allowed = (key_pos[None, :] <= group_pos[:, None])[None]
    block_max = jnp.max(jnp.where(allowed, scores, neg_large), axis=2)
    new_max = jnp.maximum(run_max, block_max)
    factor = jnp.exp(run_max - new_max)
    weights = jnp.where(allowed, jnp.exp(scores - new_max[:, :, None]), 0.0)
    new_total = run_total * factor + jnp.sum(weights, axis=2)
    new_accum = run_accum * factor[:, :, None] + jnp.einsum(
        "hts,shd->htd",
        weights.astype(jnp.bfloat16),
        value_block,
        preferred_element_type=jnp.float32,
    )
    return (new_max, new_total, new_accum)


def attention(q_attn, k_attn, v_attn, my_index, tok_rows):
    heads_local = q_attn.shape[1] // HD
    score_scale = HD ** (-0.5)
    queries = q_attn.reshape(tok_rows, heads_local, HD)
    group_list = [(queries, my_index * tok_rows + jnp.arange(tok_rows, dtype=jnp.int32))]
    initial = tuple(
        (
            (
                jnp.full((heads_local, entry[0].shape[0]), neg_large, jnp.float32),
                jnp.zeros((heads_local, entry[0].shape[0]), jnp.float32),
                jnp.zeros((heads_local, entry[0].shape[0], HD), jnp.float32),
            )
            for entry in group_list
        )
    )
    key_piece = lax.all_gather(k_attn, "ctx", axis=0, tiled=True)
    value_piece = lax.all_gather(v_attn, "ctx", axis=0, tiled=True)
    count_blocks = key_piece.shape[0] // tok_rows
    keys_split = key_piece.reshape(count_blocks, tok_rows, heads_local, HD)
    values_split = value_piece.reshape(count_blocks, tok_rows, heads_local, HD)

    def one_block(carry, item):
        key_block, value_block, block_number = item
        block_first = block_number * tok_rows
        key_pos = block_first + jnp.arange(tok_rows, dtype=jnp.int32)
        updated = []
        for entry, group_state in zip(group_list, carry):
            step_fn = partial(
                attend_block, entry[0], entry[1], key_block, value_block, key_pos, score_scale
            )
            updated.append(lax.cond(block_first <= entry[1][-1], step_fn, keep_same, group_state))
        return (tuple(updated), None)

    new_state, unused = lax.scan(
        one_block, initial, (keys_split, values_split, jnp.arange(count_blocks, dtype=jnp.int32))
    )
    outputs = [
        (state[2] / state[1][:, :, None]).transpose(1, 0, 2).astype(jnp.bfloat16)
        for state in new_state
    ]
    merged = outputs[0]
    return merged.reshape(tok_rows, heads_local * HD)


def local_general(q_conv, k_conv, v_conv, conv_filter, q_attn, k_attn, v_attn, w_conv_out, w_attn_out):
    count_ctx = lax.axis_size("ctx")
    my_index = lax.axis_index("ctx")
    tok_rows = q_conv.shape[0]
    gated = (k_conv.astype(jnp.float32) * v_conv.astype(jnp.float32)).astype(jnp.bfloat16)
    conv = spectral_conv(gated, conv_filter, my_index, tok_rows, count_ctx)
    mixed = (q_conv.astype(jnp.float32) * conv.astype(jnp.float32)).astype(jnp.bfloat16)
    attended = attention(q_attn, k_attn, v_attn, my_index, tok_rows)
    return lax.psum_scatter(
        (
            jnp.dot(mixed, w_conv_out, preferred_element_type=jnp.float32)
            + jnp.dot(attended, w_attn_out, preferred_element_type=jnp.float32)
        ).astype(jnp.bfloat16),
        "ch",
        scatter_dimension=0,
        tiled=True,
    )


GROUP = 16
TILE = 256
HALF = 128
MESH = pl.DeviceIdType.MESH


def fused_kernel(
    count_ctx, rows, width,
    qc_hbm, kc_hbm, vc_hbm, filt_ref, q_ref, k_ref, v_ref, w1_hbm, w2_hbm,
    out_ref,
    qc, kc, vc, filt,
    gated, filt_in, gated_in, q_in, k_in, v_in, conv_out, attn_out, conv_back, attn_back,
    fpad, x_turned, y_turned, stage, lhs_conv, lhs_attn, attn_part, w1, w2,
    keep, send_a, recv_a, send_b, recv_b,
    in_send, in_recv, back_send, back_recv, load_sem, a_send, a_recv, b_send, b_recv,
):
    me = lax.axis_index("ctx")
    ch = lax.axis_index("ch")
    core = lax.rem(ch, 2)
    pair = ch // 2
    core_peer = pair * 2 + (1 - core)
    pair_peer = (1 - pair) * 2 + core
    tokens = count_ctx * rows
    tiles = tokens // TILE
    groups = HD // GROUP
    my_rows = pl.ds(pl.multiple_of(me * rows, 16), rows)
    my_cols = pl.ds(pl.multiple_of(me * HD, HD), HD)
    my_groups = pl.ds(pl.multiple_of(me * groups, groups), groups)

    barrier = pltpu.get_barrier_semaphore()
    for k in range(1, count_ctx):
        peer = lax.rem(me + k, count_ctx)
        pl.semaphore_signal(barrier, inc=1, device_id=(peer, ch), device_id_type=MESH)
    pl.semaphore_signal(barrier, inc=1, device_id=(me, core_peer), device_id_type=MESH)
    pl.semaphore_signal(barrier, inc=1, device_id=(me, pair_peer), device_id_type=MESH)

    heads = ((q_ref, q_in), (k_ref, k_in), (v_ref, v_in))
    kc_copy = pltpu.make_async_copy(kc_hbm, kc, load_sem.at[0])
    vc_copy = pltpu.make_async_copy(vc_hbm, vc, load_sem.at[1])
    own_copies = [
        pltpu.make_async_copy(source.at[:, my_cols], target.at[my_rows, :], load_sem.at[2 + n])
        for n, (source, target) in enumerate(heads)
    ]
    qc_copy = pltpu.make_async_copy(qc_hbm, qc, load_sem.at[5])
    w1_copy = pltpu.make_async_copy(w1_hbm, w1, load_sem.at[6])
    w2_copy = pltpu.make_async_copy(w2_hbm, w2, load_sem.at[7])
    kc_copy.start()
    vc_copy.start()
    filt[...] = jnp.zeros_like(filt)
    filt[:, 0:rows] = filt_ref[...].astype(jnp.float32)
    pl.semaphore_wait(barrier, count_ctx + 1)

    inbound = [[] for unused in range(5)]

    def spread(source, target, number):
        for k in range(1, count_ctx):
            peer = lax.rem(me + k, count_ctx)
            peer_cols = pl.ds(pl.multiple_of(peer * HD, HD), HD)
            copy = pltpu.make_async_remote_copy(
                src_ref=source.at[:, peer_cols],
                dst_ref=target.at[my_rows, :],
                send_sem=in_send.at[number, k],
                recv_sem=in_recv.at[number, k],
                device_id=(peer, ch),
                device_id_type=MESH,
            )
            copy.start()
            inbound[number].append(copy)

    for k in range(1, count_ctx):
        peer = lax.rem(me + k, count_ctx)
        peer_groups = pl.ds(pl.multiple_of(peer * groups, groups), groups)
        copy = pltpu.make_async_remote_copy(
            src_ref=filt.at[peer_groups, :],
            dst_ref=filt_in.at[me],
            send_sem=in_send.at[4, k],
            recv_sem=in_recv.at[4, k],
            device_id=(peer, ch),
            device_id_type=MESH,
        )
        copy.start()
        inbound[4].append(copy)
    for number, (source, target) in enumerate(heads):
        spread(source, target, number + 1)
    for copy in own_copies + [qc_copy, w1_copy, w2_copy]:
        copy.start()
    kc_copy.wait()
    vc_copy.wait()
    gated[...] = (kc[...].astype(jnp.float32) * vc[...].astype(jnp.float32)).astype(jnp.bfloat16)
    spread(gated, gated_in, 0)
    gated_in[my_rows, :] = gated[:, my_cols]
    filt_in[pl.ds(me, 1)] = filt[my_groups, :].reshape(1, groups, filt.shape[1])

    def send_back(source, target, number, first, count):
        copies = []
        here = pl.ds(pl.multiple_of(first, 16), count)
        for k in range(1, count_ctx):
            peer = lax.rem(me + k, count_ctx)
            peer_rows = pl.ds(pl.multiple_of(peer * rows + first, 16), count)
            copy = pltpu.make_async_remote_copy(
                src_ref=source.at[peer_rows, :],
                dst_ref=target.at[here, my_cols],
                send_sem=back_send.at[number, k],
                recv_sem=back_recv.at[number, k],
                device_id=(peer, ch),
                device_id_type=MESH,
            )
            copy.start()
            copies.append(copy)
        kept_rows = pl.ds(pl.multiple_of(me * rows + first, 16), count)
        target[here, my_cols] = source[kept_rows, :]
        return copies

    for copy in own_copies:
        copy.wait()
    for number in (1, 2, 3):
        for copy in inbound[number]:
            copy.wait_recv()
    factor = HD ** (-0.5) * math.log2(math.e)
    below = lax.broadcasted_iota(jnp.int32, (TILE, TILE), 1) <= lax.broadcasted_iota(
        jnp.int32, (TILE, TILE), 0
    )
    for i in range(tiles):
        query = q_in[i * TILE : (i + 1) * TILE, :]
        scores = lax.dot_general(
            query,
            k_in[0 : (i + 1) * TILE, :],
            (((1,), (1,)), ((), ())),
            preferred_element_type=jnp.float32,
        )
        corner = jnp.where(below, scores[:, i * TILE :], neg_large)
        if i:
            scores = jnp.concatenate([scores[:, : i * TILE], corner], axis=1)
        else:
            scores = corner
        row_max = jnp.max(scores, axis=1, keepdims=True)
        weights = jnp.exp2((scores - row_max) * factor)
        totals = jnp.sum(weights, axis=1, keepdims=True)
        summed = jnp.dot(
            weights.astype(jnp.bfloat16),
            v_in[0 : (i + 1) * TILE, :],
            preferred_element_type=jnp.float32,
        )
        attn_out[i * TILE : (i + 1) * TILE, :] = (summed / totals).astype(jnp.bfloat16)
    attn_copies = send_back(attn_out, attn_back, 0, 0, rows)

    for copy in inbound[4]:
        copy.wait_recv()
    fpad[...] = jnp.zeros_like(fpad)
    wide = filt.shape[1]
    for j in range(count_ctx):
        first = HALF + j * rows
        base = first // HALF * HALF
        piece = jnp.concatenate(
            [filt_in[j], jnp.zeros((groups, HALF), jnp.float32)], axis=1
        )
        if first % HALF:
            piece = pltpu.roll(piece, first % HALF, 1)
        fpad[:, base : base + wide + HALF] += piece

    for copy in inbound[0]:
        copy.wait_recv()
    for j in range(tiles):
        turned = (
            gated_in[j * TILE : (j + 1) * TILE, :].astype(jnp.float32).T.astype(jnp.bfloat16)
        )
        for g in range(groups):
            x_turned[g, j * GROUP : (j + 1) * GROUP, :] = turned[g * GROUP : (g + 1) * GROUP, :]

    span = tokens + HALF

    def one_group(g, carry):
        line = fpad[pl.ds(g, 1), 0 : span + HALF]
        shifted = pltpu.roll(
            jnp.broadcast_to(line, (HALF, span + HALF)), 0, 1, stride=1, stride_axis=0
        ).astype(jnp.bfloat16)
        for d in range(tiles):
            block = jnp.concatenate(
                [
                    shifted[:, HALF + d * TILE : HALF + (d + 1) * TILE],
                    shifted[:, d * TILE : (d + 1) * TILE],
                ],
                axis=0,
            )
            part = jnp.dot(
                x_turned[g, 0 : (tiles - d) * GROUP, :], block, preferred_element_type=jnp.float32
            )
            if d == 0:
                y_turned[g] = part
            else:
                y_turned[g, d * GROUP :, :] += part
        return carry

    lax.fori_loop(0, groups, one_group, 0)
    for i in range(tiles):
        gathered = y_turned[:, i * GROUP : (i + 1) * GROUP, :].reshape(HD, TILE)
        conv_out[i * TILE : (i + 1) * TILE, :] = gathered.T.astype(jnp.bfloat16)
    half = rows // 2
    halves = (half * (1 - pair), half * pair)
    conv_copies = [
        send_back(conv_out, conv_back, 1 + n, first, half) for n, first in enumerate(halves)
    ]

    share = rows // 4
    padded = keep.shape[1]
    chunk = keep.shape[2]
    chunks = keep.shape[0] // 2

    def place(target, base):
        for slot, owner in enumerate((core, 1 - core)):
            part = stage[pl.ds(pl.multiple_of(owner * share, 8), share), :]
            filler = jnp.zeros((padded - share, width), jnp.float32)
            target[base + slot * padded : base + (slot + 1) * padded, :] = jnp.concatenate(
                [part, filler], axis=0
            ).astype(jnp.bfloat16)

    def take(first):
        here = pl.ds(pl.multiple_of(first, 16), half)
        stage[...] = qc[here, :].astype(jnp.float32) * conv_back[here, :].astype(jnp.float32)
        place(lhs_conv, 0)

    def copy_a(n):
        return pltpu.make_async_remote_copy(
            src_ref=send_a.at[n],
            dst_ref=recv_a.at[n],
            send_sem=a_send.at[n],
            recv_sem=a_recv.at[n],
            device_id=(me, core_peer),
            device_id_type=MESH,
        )

    def copy_b(n):
        return pltpu.make_async_remote_copy(
            src_ref=send_b.at[n],
            dst_ref=recv_b.at[n],
            send_sem=b_send.at[n],
            recv_sem=b_recv.at[n],
            device_id=(me, pair_peer),
            device_id_type=MESH,
        )

    def project_attn(n, carry):
        cols = pl.ds(pl.multiple_of(n * chunk, chunk), chunk)
        attn_part[n] = jnp.dot(lhs_attn[...], w2[:, cols], preferred_element_type=jnp.float32)
        return carry

    def project(n, base):
        cols = pl.ds(pl.multiple_of(n * chunk, chunk), chunk)
        row = 2 * padded if base else 0
        total = (
            jnp.dot(lhs_conv[...], w1[:, cols], preferred_element_type=jnp.float32)
            + attn_part[n, row : row + 2 * padded, :]
        )
        keep[base + n] = total[0:padded]
        send_a[base + n] = total[padded:].astype(jnp.bfloat16)
        copy_a(base + n).start()

    def forward(n):
        copy_a(n).wait_recv()
        send_b[n] = (keep[n] + recv_a[n].astype(jnp.float32)).astype(jnp.bfloat16)
        copy_b(n).start()

    for copy in (qc_copy, w1_copy, w2_copy):
        copy.wait()
    for copy in attn_copies:
        copy.wait_recv()
    for n, first in enumerate(halves):
        stage[...] = attn_back[pl.ds(pl.multiple_of(first, 16), half), :].astype(jnp.float32)
        place(lhs_attn, 2 * n * padded)
    lax.fori_loop(0, chunks, project_attn, 0)
    for copy in conv_copies[0]:
        copy.wait_recv()
    take(halves[0])
    project(0, 0)

    def first_half(n, carry):
        project(n, 0)
        forward(n - 1)
        return carry

    lax.fori_loop(1, chunks, first_half, 0)
    forward(chunks - 1)
    for copy in conv_copies[1]:
        copy.wait_recv()
    take(halves[1])

    def second_half(n, carry):
        project(n, chunks)
        return carry

    lax.fori_loop(0, chunks, second_half, 0)

    def finish(n, carry):
        cols = pl.ds(pl.multiple_of(n * chunk, chunk), chunk)
        copy_a(chunks + n).wait_recv()
        copy_b(n).wait_recv()
        total = (
            keep[chunks + n]
            + recv_a[chunks + n].astype(jnp.float32)
            + recv_b[n].astype(jnp.float32)
        )
        out_ref[:, cols] = total[0:share].astype(jnp.bfloat16)
        copy_a(n).wait_send()
        copy_a(chunks + n).wait_send()
        copy_b(n).wait_send()
        return carry

    lax.fori_loop(0, chunks, finish, 0)
    for copies in inbound + conv_copies + [attn_copies]:
        for copy in copies:
            copy.wait_send()


def local_fused(q_conv, k_conv, v_conv, conv_filter, q_attn, k_attn, v_attn, w_conv_out, w_attn_out):
    count_ctx = lax.axis_size("ctx")
    rows, width = q_conv.shape
    dout = w_conv_out.shape[1]
    tokens = count_ctx * rows
    groups = HD // GROUP
    wide = (rows + HALF - 1) // HALF * HALF
    share = rows // 4
    padded = (share + 15) // 16 * 16
    chunk = 512
    chunks = dout // chunk
    tiles = tokens // TILE
    bf16, f32 = jnp.bfloat16, jnp.float32
    vmem = pl.BlockSpec(memory_space=pltpu.VMEM)
    hbm = pl.BlockSpec(memory_space=pl.ANY)
    dma = pltpu.SemaphoreType.DMA
    return pl.pallas_call(
        partial(fused_kernel, count_ctx, rows, width),
        out_shape=jax.ShapeDtypeStruct((share, dout), bf16),
        in_specs=[hbm] * 3 + [vmem] + [hbm] * 5,
        out_specs=vmem,
        scratch_shapes=[
            pltpu.VMEM((rows, width), bf16),
            pltpu.VMEM((rows, width), bf16),
            pltpu.VMEM((rows, width), bf16),
            pltpu.VMEM((conv_filter.shape[1], wide), f32),
            pltpu.VMEM((rows, width), bf16),
            pltpu.VMEM((count_ctx, groups, wide), f32),
            pltpu.VMEM((tokens, HD), bf16),
            pltpu.VMEM((tokens, HD), bf16),
            pltpu.VMEM((tokens, HD), bf16),
            pltpu.VMEM((tokens, HD), bf16),
            pltpu.VMEM((tokens, HD), bf16),
            pltpu.VMEM((tokens, HD), bf16),
            pltpu.VMEM((rows, width), bf16),
            pltpu.VMEM((rows, width), bf16),
            pltpu.VMEM((groups, tokens + 2 * HALF + TILE), f32),
            pltpu.VMEM((groups, tiles * GROUP, TILE), bf16),
            pltpu.VMEM((groups, tiles * GROUP, TILE), f32),
            pltpu.VMEM((rows // 2, width), f32),
            pltpu.VMEM((2 * padded, width), bf16),
            pltpu.VMEM((4 * padded, width), bf16),
            pltpu.VMEM((chunks, 4 * padded, chunk), f32),
            pltpu.VMEM(w_conv_out.shape, bf16),
            pltpu.VMEM(w_attn_out.shape, bf16),
            pltpu.VMEM((2 * chunks, padded, chunk), f32),
            pltpu.VMEM((2 * chunks, padded, chunk), bf16),
            pltpu.VMEM((2 * chunks, padded, chunk), bf16),
            pltpu.VMEM((chunks, padded, chunk), bf16),
            pltpu.VMEM((chunks, padded, chunk), bf16),
            dma((5, count_ctx)),
            dma((5, count_ctx)),
            dma((3, count_ctx)),
            dma((3, count_ctx)),
            dma((8,)),
            dma((2 * chunks,)),
            dma((2 * chunks,)),
            dma((chunks,)),
            dma((chunks,)),
        ],
        compiler_params=pltpu.CompilerParams(
            collective_id=0, has_side_effects=True, vmem_limit_bytes=56 * 1024 * 1024
        ),
        name="fused_block",
    )(q_conv, k_conv, v_conv, conv_filter.T, q_attn, k_attn, v_attn, w_conv_out, w_attn_out)


def local(q_conv, k_conv, v_conv, conv_filter, q_attn, k_attn, v_attn, w_conv_out, w_attn_out):
    count_ctx = lax.axis_size("ctx")
    rows, width = q_conv.shape
    dout = w_conv_out.shape[1]
    fits = (
        width == count_ctx * HD
        and conv_filter.shape[1] * GROUP == width
        and lax.axis_size("ch") == 4
        and rows % 32 == 0
        and (count_ctx * rows) % TILE == 0
        and count_ctx * rows <= 2048
        and dout % 512 == 0
    )
    chosen = local_fused if fits else local_general
    return chosen(
        q_conv, k_conv, v_conv, conv_filter, q_attn, k_attn, v_attn, w_conv_out, w_attn_out
    )


def solution(mesh):
    return jax.shard_map(
        local,
        mesh=mesh,
        in_specs=(
            P("ctx", "ch"),
            P("ctx", "ch"),
            P("ctx", "ch"),
            P("ctx", "ch"),
            P("ctx", "ch"),
            P("ctx", "ch"),
            P("ctx", "ch"),
            P("ch", None),
            P("ch", None),
        ),
        out_specs=P(("ctx", "ch"), None),
        check_vma=False,
    )
```

```python
from functools import partial
import math

import jax
import jax.numpy as jnp
from jax import lax
from jax.experimental import pallas as pl
from jax.experimental.pallas import tpu as pltpu
from jax.sharding import PartitionSpec as P

HD = 128


two_pi = 2.0 * math.pi
neg_large = -1e30
highest = lax.Precision.HIGHEST


def angle_table(left_idx, right_idx, period):
    product = left_idx[:, None] * right_idx[None, :] % period
    return product.astype(jnp.float32) * (two_pi / period)


def section_coarse(values, cos_table, sin_table, twiddle):
    real_part = jnp.einsum("kn,nsc->ksc", cos_table, values, precision=highest)
    imag_part = -jnp.einsum("kn,nsc->ksc", sin_table, values, precision=highest)
    cos_twist = jnp.cos(twiddle)[:, :, None]
    sin_twist = jnp.sin(twiddle)[:, :, None]
    return (
        real_part * cos_twist + imag_part * sin_twist,
        imag_part * cos_twist - real_part * sin_twist,
    )


def section_fine(real_part, imag_part, cos_table, sin_table, direction):
    cos_real = jnp.einsum("kn,anc->akc", cos_table, real_part, precision=highest)
    cos_imag = jnp.einsum("kn,anc->akc", cos_table, imag_part, precision=highest)
    sin_real = jnp.einsum("kn,anc->akc", sin_table, real_part, precision=highest)
    sin_imag = jnp.einsum("kn,anc->akc", sin_table, imag_part, precision=highest)
    return (cos_real - direction * sin_imag, cos_imag + direction * sin_real)


def spectral_conv(gated, filters, my_index, tok_rows, count_ctx):
    chans = gated.shape[1]
    groups = filters.shape[1]
    share = chans // groups
    sub_rows = tok_rows // count_ctx
    period = 2 * count_ctx * tok_rows
    got_source, got_filter = (
        lax.all_to_all(
            gated.reshape(1, tok_rows, chans), "ctx", split_axis=1, concat_axis=0, tiled=True
        ),
        lax.all_to_all(
            filters.reshape(1, tok_rows, groups), "ctx", split_axis=1, concat_axis=0, tiled=True
        ),
    )
    coarse_idx = jnp.arange(count_ctx, dtype=jnp.int32)
    coarse_freq = jnp.arange(2 * count_ctx, dtype=jnp.int32)
    coarse_angle = angle_table(coarse_freq, coarse_idx, 2 * count_ctx)
    cos_coarse = jnp.cos(coarse_angle)
    sin_coarse = jnp.sin(coarse_angle)
    fine_global = my_index * sub_rows + jnp.arange(sub_rows, dtype=jnp.int32)
    twist_in = angle_table(coarse_freq, fine_global, period)
    source_re, source_im = section_coarse(
        got_source.astype(jnp.float32), cos_coarse, sin_coarse, twist_in
    )
    filter_re, filter_im = section_coarse(
        got_filter.astype(jnp.float32), cos_coarse, sin_coarse, twist_in
    )
    source_re, source_im, filter_re, filter_im = (
        lax.all_to_all(
            source_re.astype(jnp.bfloat16), "ctx", split_axis=0, concat_axis=1, tiled=True
        ).astype(source_re.dtype),
        lax.all_to_all(
            source_im.astype(jnp.bfloat16), "ctx", split_axis=0, concat_axis=1, tiled=True
        ).astype(source_im.dtype),
        lax.all_to_all(
            filter_re.astype(jnp.bfloat16), "ctx", split_axis=0, concat_axis=1, tiled=True
        ).astype(filter_re.dtype),
        lax.all_to_all(
            filter_im.astype(jnp.bfloat16), "ctx", split_axis=0, concat_axis=1, tiled=True
        ).astype(filter_im.dtype),
    )
    fine_idx = jnp.arange(tok_rows, dtype=jnp.int32)
    fine_angle = angle_table(fine_idx, fine_idx, tok_rows)
    cos_fine = jnp.cos(fine_angle)
    sin_fine = jnp.sin(fine_angle)
    source_re, source_im = section_fine(source_re, source_im, cos_fine, sin_fine, -1.0)
    filter_re, filter_im = section_fine(filter_re, filter_im, cos_fine, sin_fine, -1.0)
    split_re = source_re.reshape(2, tok_rows, groups, share)
    split_im = source_im.reshape(2, tok_rows, groups, share)
    prod_re = split_re * filter_re[..., None] - split_im * filter_im[..., None]
    prod_im = split_re * filter_im[..., None] + split_im * filter_re[..., None]
    back_re, back_im = section_fine(
        prod_re.reshape(2, tok_rows, chans),
        prod_im.reshape(2, tok_rows, chans),
        cos_fine,
        sin_fine,
        1.0,
    )
    pair_freq = my_index * 2 + jnp.arange(2, dtype=jnp.int32)
    twist_out = angle_table(pair_freq, fine_idx, period)
    cos_out = jnp.cos(twist_out)[:, :, None]
    sin_out = jnp.sin(twist_out)[:, :, None]
    turned_re = back_re * cos_out - back_im * sin_out
    turned_im = back_re * sin_out + back_im * cos_out
    turned_re, turned_im = (
        lax.all_to_all(
            turned_re.astype(jnp.bfloat16), "ctx", split_axis=1, concat_axis=0, tiled=True
        ).astype(turned_re.dtype),
        lax.all_to_all(
            turned_im.astype(jnp.bfloat16), "ctx", split_axis=1, concat_axis=0, tiled=True
        ).astype(turned_im.dtype),
    )
    result = jnp.einsum("nk,ksc->nsc", cos_coarse.T, turned_re, precision=highest)
    result = result - jnp.einsum("nk,ksc->nsc", sin_coarse.T, turned_im, precision=highest)
    rounded = (result / period).astype(jnp.bfloat16)
    returned = lax.all_to_all(rounded, "ctx", split_axis=0, concat_axis=1, tiled=True)
    return returned.reshape(tok_rows, chans)


def keep_same(running):
    return running


def attend_block(group_query, group_pos, key_block, value_block, key_pos, score_scale, group_state):
    run_max, run_total, run_accum = group_state
    scores = (
        jnp.einsum("thd,shd->hts", group_query, key_block, preferred_element_type=jnp.float32)
        * score_scale
    )
    allowed = (key_pos[None, :] <= group_pos[:, None])[None]
    block_max = jnp.max(jnp.where(allowed, scores, neg_large), axis=2)
    new_max = jnp.maximum(run_max, block_max)
    factor = jnp.exp(run_max - new_max)
    weights = jnp.where(allowed, jnp.exp(scores - new_max[:, :, None]), 0.0)
    new_total = run_total * factor + jnp.sum(weights, axis=2)
    new_accum = run_accum * factor[:, :, None] + jnp.einsum(
        "hts,shd->htd",
        weights.astype(jnp.bfloat16),
        value_block,
        preferred_element_type=jnp.float32,
    )
    return (new_max, new_total, new_accum)


def attention(q_attn, k_attn, v_attn, my_index, tok_rows):
    heads_local = q_attn.shape[1] // HD
    score_scale = HD ** (-0.5)
    queries = q_attn.reshape(tok_rows, heads_local, HD)
    group_list = [(queries, my_index * tok_rows + jnp.arange(tok_rows, dtype=jnp.int32))]
    initial = tuple(
        (
            (
                jnp.full((heads_local, entry[0].shape[0]), neg_large, jnp.float32),
                jnp.zeros((heads_local, entry[0].shape[0]), jnp.float32),
                jnp.zeros((heads_local, entry[0].shape[0], HD), jnp.float32),
            )
            for entry in group_list
        )
    )
    key_piece = lax.all_gather(k_attn, "ctx", axis=0, tiled=True)
    value_piece = lax.all_gather(v_attn, "ctx", axis=0, tiled=True)
    count_blocks = key_piece.shape[0] // tok_rows
    keys_split = key_piece.reshape(count_blocks, tok_rows, heads_local, HD)
    values_split = value_piece.reshape(count_blocks, tok_rows, heads_local, HD)

    def one_block(carry, item):
        key_block, value_block, block_number = item
        block_first = block_number * tok_rows
        key_pos = block_first + jnp.arange(tok_rows, dtype=jnp.int32)
        updated = []
        for entry, group_state in zip(group_list, carry):
            step_fn = partial(
                attend_block, entry[0], entry[1], key_block, value_block, key_pos, score_scale
            )
            updated.append(lax.cond(block_first <= entry[1][-1], step_fn, keep_same, group_state))
        return (tuple(updated), None)

    new_state, unused = lax.scan(
        one_block, initial, (keys_split, values_split, jnp.arange(count_blocks, dtype=jnp.int32))
    )
    outputs = [
        (state[2] / state[1][:, :, None]).transpose(1, 0, 2).astype(jnp.bfloat16)
        for state in new_state
    ]
    merged = outputs[0]
    return merged.reshape(tok_rows, heads_local * HD)


def local_general(q_conv, k_conv, v_conv, conv_filter, q_attn, k_attn, v_attn, w_conv_out, w_attn_out):
    count_ctx = lax.axis_size("ctx")
    my_index = lax.axis_index("ctx")
    tok_rows = q_conv.shape[0]
    gated = (k_conv.astype(jnp.float32) * v_conv.astype(jnp.float32)).astype(jnp.bfloat16)
    conv = spectral_conv(gated, conv_filter, my_index, tok_rows, count_ctx)
    mixed = (q_conv.astype(jnp.float32) * conv.astype(jnp.float32)).astype(jnp.bfloat16)
    attended = attention(q_attn, k_attn, v_attn, my_index, tok_rows)
    return lax.psum_scatter(
        (
            jnp.dot(mixed, w_conv_out, preferred_element_type=jnp.float32)
            + jnp.dot(attended, w_attn_out, preferred_element_type=jnp.float32)
        ).astype(jnp.bfloat16),
        "ch",
        scatter_dimension=0,
        tiled=True,
    )


GROUP = 16
TILE = 256
HALF = 128
MESH = pl.DeviceIdType.MESH


def fused_kernel(
    count_ctx, rows, width,
    qc_hbm, kc_hbm, vc_hbm, filt_ref, q_ref, k_ref, v_ref, w1_hbm, w2_hbm,
    out_ref,
    qc, kc, vc, filt,
    gated, filt_in, gated_in, q_in, k_in, v_in, conv_out, attn_out, conv_back, attn_back,
    fpad, x_turned, y_turned, stage, lhs_conv, lhs_attn, w1, w2,
    keep, send_a, recv_a, send_b, recv_b,
    in_send, in_recv, back_send, back_recv, load_sem, a_send, a_recv, b_send, b_recv,
):
    me = lax.axis_index("ctx")
    ch = lax.axis_index("ch")
    core = lax.rem(ch, 2)
    pair = ch // 2
    core_peer = pair * 2 + (1 - core)
    pair_peer = (1 - pair) * 2 + core
    tokens = count_ctx * rows
    tiles = tokens // TILE
    groups = HD // GROUP
    my_rows = pl.ds(pl.multiple_of(me * rows, 16), rows)
    my_cols = pl.ds(pl.multiple_of(me * HD, HD), HD)
    my_groups = pl.ds(pl.multiple_of(me * groups, groups), groups)

    barrier = pltpu.get_barrier_semaphore()
    for k in range(1, count_ctx):
        peer = lax.rem(me + k, count_ctx)
        pl.semaphore_signal(barrier, inc=1, device_id=(peer, ch), device_id_type=MESH)
    pl.semaphore_signal(barrier, inc=1, device_id=(me, core_peer), device_id_type=MESH)
    pl.semaphore_signal(barrier, inc=1, device_id=(me, pair_peer), device_id_type=MESH)

    heads = ((q_ref, q_in), (k_ref, k_in), (v_ref, v_in))
    kc_copy = pltpu.make_async_copy(kc_hbm, kc, load_sem.at[0])
    vc_copy = pltpu.make_async_copy(vc_hbm, vc, load_sem.at[1])
    own_copies = [
        pltpu.make_async_copy(source.at[:, my_cols], target.at[my_rows, :], load_sem.at[2 + n])
        for n, (source, target) in enumerate(heads)
    ]
    qc_copy = pltpu.make_async_copy(qc_hbm, qc, load_sem.at[5])
    w1_copy = pltpu.make_async_copy(w1_hbm, w1, load_sem.at[6])
    w2_copy = pltpu.make_async_copy(w2_hbm, w2, load_sem.at[7])
    kc_copy.start()
    vc_copy.start()
    filt[...] = jnp.zeros_like(filt)
    filt[:, 0:rows] = filt_ref[...].astype(jnp.float32)
    pl.semaphore_wait(barrier, count_ctx + 1)

    inbound = [[] for unused in range(5)]

    def spread(source, target, number):
        for k in range(1, count_ctx):
            peer = lax.rem(me + k, count_ctx)
            peer_cols = pl.ds(pl.multiple_of(peer * HD, HD), HD)
            copy = pltpu.make_async_remote_copy(
                src_ref=source.at[:, peer_cols],
                dst_ref=target.at[my_rows, :],
                send_sem=in_send.at[number, k],
                recv_sem=in_recv.at[number, k],
                device_id=(peer, ch),
                device_id_type=MESH,
            )
            copy.start()
            inbound[number].append(copy)

    for k in range(1, count_ctx):
        peer = lax.rem(me + k, count_ctx)
        peer_groups = pl.ds(pl.multiple_of(peer * groups, groups), groups)
        copy = pltpu.make_async_remote_copy(
            src_ref=filt.at[peer_groups, :],
            dst_ref=filt_in.at[me],
            send_sem=in_send.at[4, k],
            recv_sem=in_recv.at[4, k],
            device_id=(peer, ch),
            device_id_type=MESH,
        )
        copy.start()
        inbound[4].append(copy)
    for number, (source, target) in enumerate(heads):
        spread(source, target, number + 1)
    for copy in own_copies + [qc_copy, w1_copy, w2_copy]:
        copy.start()
    kc_copy.wait()
    vc_copy.wait()
    gated[...] = (kc[...].astype(jnp.float32) * vc[...].astype(jnp.float32)).astype(jnp.bfloat16)
    spread(gated, gated_in, 0)
    gated_in[my_rows, :] = gated[:, my_cols]
    filt_in[pl.ds(me, 1)] = filt[my_groups, :].reshape(1, groups, filt.shape[1])

    def send_back(source, target, number, first, count):
        copies = []
        here = pl.ds(pl.multiple_of(first, 16), count)
        for k in range(1, count_ctx):
            peer = lax.rem(me + k, count_ctx)
            peer_rows = pl.ds(pl.multiple_of(peer * rows + first, 16), count)
            copy = pltpu.make_async_remote_copy(
                src_ref=source.at[peer_rows, :],
                dst_ref=target.at[here, my_cols],
                send_sem=back_send.at[number, k],
                recv_sem=back_recv.at[number, k],
                device_id=(peer, ch),
                device_id_type=MESH,
            )
            copy.start()
            copies.append(copy)
        kept_rows = pl.ds(pl.multiple_of(me * rows + first, 16), count)
        target[here, my_cols] = source[kept_rows, :]
        return copies

    for copy in own_copies:
        copy.wait()
    for number in (1, 2, 3):
        for copy in inbound[number]:
            copy.wait_recv()
    factor = HD ** (-0.5) * math.log2(math.e)
    below = lax.broadcasted_iota(jnp.int32, (TILE, TILE), 1) <= lax.broadcasted_iota(
        jnp.int32, (TILE, TILE), 0
    )
    for i in range(tiles):
        query = q_in[i * TILE : (i + 1) * TILE, :]
        scores = lax.dot_general(
            query,
            k_in[0 : (i + 1) * TILE, :],
            (((1,), (1,)), ((), ())),
            preferred_element_type=jnp.float32,
        )
        corner = jnp.where(below, scores[:, i * TILE :], neg_large)
        if i:
            scores = jnp.concatenate([scores[:, : i * TILE], corner], axis=1)
        else:
            scores = corner
        row_max = jnp.max(scores, axis=1, keepdims=True)
        weights = jnp.exp2((scores - row_max) * factor)
        totals = jnp.sum(weights, axis=1, keepdims=True)
        summed = jnp.dot(
            weights.astype(jnp.bfloat16),
            v_in[0 : (i + 1) * TILE, :],
            preferred_element_type=jnp.float32,
        )
        attn_out[i * TILE : (i + 1) * TILE, :] = (summed / totals).astype(jnp.bfloat16)
    half = rows // 2
    halves = (half * (1 - pair), half * pair)
    early_copies = send_back(attn_out, attn_back, 0, halves[0], half)

    for copy in inbound[4]:
        copy.wait_recv()
    fpad[...] = jnp.zeros_like(fpad)
    wide = filt.shape[1]
    for j in range(count_ctx):
        first = HALF + j * rows
        base = first // HALF * HALF
        piece = jnp.concatenate(
            [filt_in[j], jnp.zeros((groups, HALF), jnp.float32)], axis=1
        )
        if first % HALF:
            piece = pltpu.roll(piece, first % HALF, 1)
        fpad[:, base : base + wide + HALF] += piece

    for copy in inbound[0]:
        copy.wait_recv()
    for j in range(tiles):
        turned = (
            gated_in[j * TILE : (j + 1) * TILE, :].astype(jnp.float32).T.astype(jnp.bfloat16)
        )
        for g in range(groups):
            x_turned[g, j * GROUP : (j + 1) * GROUP, :] = turned[g * GROUP : (g + 1) * GROUP, :]

    span = tokens + HALF

    def one_group(g, carry):
        line = fpad[pl.ds(g, 1), 0 : span + HALF]
        shifted = pltpu.roll(
            jnp.broadcast_to(line, (HALF, span + HALF)), 0, 1, stride=1, stride_axis=0
        ).astype(jnp.bfloat16)
        for d in range(tiles):
            block = jnp.concatenate(
                [
                    shifted[:, HALF + d * TILE : HALF + (d + 1) * TILE],
                    shifted[:, d * TILE : (d + 1) * TILE],
                ],
                axis=0,
            )
            part = jnp.dot(
                x_turned[g, 0 : (tiles - d) * GROUP, :], block, preferred_element_type=jnp.float32
            )
            if d == 0:
                y_turned[g] = part
            else:
                y_turned[g, d * GROUP :, :] += part
        return carry

    lax.fori_loop(0, groups, one_group, 0)
    for i in range(tiles):
        gathered = y_turned[:, i * GROUP : (i + 1) * GROUP, :].reshape(HD, TILE)
        conv_out[i * TILE : (i + 1) * TILE, :] = gathered.T.astype(jnp.bfloat16)
    early_copies += send_back(conv_out, conv_back, 1, halves[0], half)
    late_copies = send_back(attn_out, attn_back, 2, halves[1], half)
    late_copies += send_back(conv_out, conv_back, 3, halves[1], half)

    share = rows // 4
    padded = keep.shape[1]
    chunk = keep.shape[2]
    chunks = keep.shape[0] // 2

    def place(target):
        for slot, owner in enumerate((core, 1 - core)):
            part = stage[pl.ds(pl.multiple_of(owner * share, 8), share), :]
            filler = jnp.zeros((padded - share, width), jnp.float32)
            target[slot * padded : (slot + 1) * padded, :] = jnp.concatenate(
                [part, filler], axis=0
            ).astype(jnp.bfloat16)

    def take(first):
        here = pl.ds(pl.multiple_of(first, 16), half)
        stage[...] = qc[here, :].astype(jnp.float32) * conv_back[here, :].astype(jnp.float32)
        place(lhs_conv)
        stage[...] = attn_back[here, :].astype(jnp.float32)
        place(lhs_attn)

    def copy_a(n):
        return pltpu.make_async_remote_copy(
            src_ref=send_a.at[n],
            dst_ref=recv_a.at[n],
            send_sem=a_send.at[n],
            recv_sem=a_recv.at[n],
            device_id=(me, core_peer),
            device_id_type=MESH,
        )

    def copy_b(n):
        return pltpu.make_async_remote_copy(
            src_ref=send_b.at[n],
            dst_ref=recv_b.at[n],
            send_sem=b_send.at[n],
            recv_sem=b_recv.at[n],
            device_id=(me, pair_peer),
            device_id_type=MESH,
        )

    def project(n, base):
        cols = pl.ds(pl.multiple_of(n * chunk, chunk), chunk)
        total = jnp.dot(
            lhs_conv[...], w1[:, cols], preferred_element_type=jnp.float32
        ) + jnp.dot(lhs_attn[...], w2[:, cols], preferred_element_type=jnp.float32)
        keep[base + n] = total[0:padded]
        send_a[base + n] = total[padded:].astype(jnp.bfloat16)
        copy_a(base + n).start()

    def forward(n):
        copy_a(n).wait_recv()
        send_b[n] = (keep[n] + recv_a[n].astype(jnp.float32)).astype(jnp.bfloat16)
        copy_b(n).start()

    for copy in (qc_copy, w1_copy, w2_copy):
        copy.wait()
    for copy in early_copies:
        copy.wait_recv()
    take(halves[0])
    project(0, 0)

    def first_half(n, carry):
        project(n, 0)
        forward(n - 1)
        return carry

    lax.fori_loop(1, chunks, first_half, 0)
    forward(chunks - 1)
    for copy in late_copies:
        copy.wait_recv()
    take(halves[1])

    def second_half(n, carry):
        project(n, chunks)
        return carry

    lax.fori_loop(0, chunks, second_half, 0)

    def finish(n, carry):
        cols = pl.ds(pl.multiple_of(n * chunk, chunk), chunk)
        copy_a(chunks + n).wait_recv()
        copy_b(n).wait_recv()
        total = (
            keep[chunks + n]
            + recv_a[chunks + n].astype(jnp.float32)
            + recv_b[n].astype(jnp.float32)
        )
        out_ref[:, cols] = total[0:share].astype(jnp.bfloat16)
        copy_a(n).wait_send()
        copy_a(chunks + n).wait_send()
        copy_b(n).wait_send()
        return carry

    lax.fori_loop(0, chunks, finish, 0)
    for copies in inbound + [early_copies, late_copies]:
        for copy in copies:
            copy.wait_send()


def local_fused(q_conv, k_conv, v_conv, conv_filter, q_attn, k_attn, v_attn, w_conv_out, w_attn_out):
    count_ctx = lax.axis_size("ctx")
    rows, width = q_conv.shape
    dout = w_conv_out.shape[1]
    tokens = count_ctx * rows
    groups = HD // GROUP
    wide = (rows + HALF - 1) // HALF * HALF
    share = rows // 4
    padded = (share + 15) // 16 * 16
    chunk = 512
    chunks = dout // chunk
    tiles = tokens // TILE
    bf16, f32 = jnp.bfloat16, jnp.float32
    vmem = pl.BlockSpec(memory_space=pltpu.VMEM)
    hbm = pl.BlockSpec(memory_space=pl.ANY)
    dma = pltpu.SemaphoreType.DMA
    return pl.pallas_call(
        partial(fused_kernel, count_ctx, rows, width),
        out_shape=jax.ShapeDtypeStruct((share, dout), bf16),
        in_specs=[hbm] * 3 + [vmem] + [hbm] * 5,
        out_specs=vmem,
        scratch_shapes=[
            pltpu.VMEM((rows, width), bf16),
            pltpu.VMEM((rows, width), bf16),
            pltpu.VMEM((rows, width), bf16),
            pltpu.VMEM((conv_filter.shape[1], wide), f32),
            pltpu.VMEM((rows, width), bf16),
            pltpu.VMEM((count_ctx, groups, wide), f32),
            pltpu.VMEM((tokens, HD), bf16),
            pltpu.VMEM((tokens, HD), bf16),
            pltpu.VMEM((tokens, HD), bf16),
            pltpu.VMEM((tokens, HD), bf16),
            pltpu.VMEM((tokens, HD), bf16),
            pltpu.VMEM((tokens, HD), bf16),
            pltpu.VMEM((rows, width), bf16),
            pltpu.VMEM((rows, width), bf16),
            pltpu.VMEM((groups, tokens + 2 * HALF + TILE), f32),
            pltpu.VMEM((groups, tiles * GROUP, TILE), bf16),
            pltpu.VMEM((groups, tiles * GROUP, TILE), f32),
            pltpu.VMEM((rows // 2, width), f32),
            pltpu.VMEM((2 * padded, width), bf16),
            pltpu.VMEM((2 * padded, width), bf16),
            pltpu.VMEM(w_conv_out.shape, bf16),
            pltpu.VMEM(w_attn_out.shape, bf16),
            pltpu.VMEM((2 * chunks, padded, chunk), f32),
            pltpu.VMEM((2 * chunks, padded, chunk), bf16),
            pltpu.VMEM((2 * chunks, padded, chunk), bf16),
            pltpu.VMEM((chunks, padded, chunk), bf16),
            pltpu.VMEM((chunks, padded, chunk), bf16),
            dma((5, count_ctx)),
            dma((5, count_ctx)),
            dma((4, count_ctx)),
            dma((4, count_ctx)),
            dma((8,)),
            dma((2 * chunks,)),
            dma((2 * chunks,)),
            dma((chunks,)),
            dma((chunks,)),
        ],
        compiler_params=pltpu.CompilerParams(
            collective_id=0, has_side_effects=True, vmem_limit_bytes=56 * 1024 * 1024
        ),
        name="fused_block",
    )(q_conv, k_conv, v_conv, conv_filter.T, q_attn, k_attn, v_attn, w_conv_out, w_attn_out)


def local(q_conv, k_conv, v_conv, conv_filter, q_attn, k_attn, v_attn, w_conv_out, w_attn_out):
    count_ctx = lax.axis_size("ctx")
    rows, width = q_conv.shape
    dout = w_conv_out.shape[1]
    fits = (
        width == count_ctx * HD
        and conv_filter.shape[1] * GROUP == width
        and lax.axis_size("ch") == 4
        and rows % 32 == 0
        and (count_ctx * rows) % TILE == 0
        and count_ctx * rows <= 2048
        and dout % 512 == 0
    )
    chosen = local_fused if fits else local_general
    return chosen(
        q_conv, k_conv, v_conv, conv_filter, q_attn, k_attn, v_attn, w_conv_out, w_attn_out
    )


def solution(mesh):
    return jax.shard_map(
        local,
        mesh=mesh,
        in_specs=(
            P("ctx", "ch"),
            P("ctx", "ch"),
            P("ctx", "ch"),
            P("ctx", "ch"),
            P("ctx", "ch"),
            P("ctx", "ch"),
            P("ctx", "ch"),
            P("ch", None),
            P("ch", None),
        ),
        out_specs=P(("ctx", "ch"), None),
        check_vma=False,
    )
```
